32 devices in a mesh: grp: 8 (over y, x, core), mem: 4 (over z).
Axes of the slice: x: 2, y: 2, z: 4, core: 2. Of those that a mesh axis runs over, the one named last changes fastest.
Arguments:
- filterbank: float32 [8, 4, 8, 16000], P('grp', 'mem'), may hold values from -6 to 6
- destination: int32 [8, 32], P('grp', 'mem'), may hold values from 0 to 7, as said below
- initial_conv_weight: bfloat16 [400, 1024], replicated, may hold values from -0.3125 to 0.3125
- expand_weight: bfloat16 [1024, 1024], replicated, may hold values from -0.1875 to 0.1875
- branch_weight: bfloat16 [7, 384, 128], replicated, may hold values from -0.3125 to 0.3125
- merge_weight: bfloat16 [1024, 1024], replicated, may hold values from -0.1875 to 0.1875
- squeeze_weight: bfloat16 [1024, 128], replicated, may hold values from -0.1875 to 0.1875
- excite_weight: bfloat16 [128, 1024], replicated, may hold values from -0.5 to 0.5
- attend_weight: bfloat16 [8, 3072, 128], P('grp'), may hold values from -0.1875 to 0.1875
- score_weight: bfloat16 [8, 128, 1024], P('grp'), may hold values from -0.5 to 0.5
- embed_weight: bfloat16 [8, 2048, 192], P('grp'), may hold values from -0.125 to 0.125
- language_weight: bfloat16 [8, 192, 107], P('grp'), may hold values from -0.4375 to 0.4375
Outputs:
- language_logits: float32 [8, 32, 107], P('grp', 'mem')
- similarity: float32 [8, 32, 32], P('grp', 'mem')
The draws below stay inside these ranges and needn't reach their ends.
Inputs may be any that keep to these rules, and one draw needn't show every extreme that they name: `destination`: each device sends its 8 segments to 8 different groups, so at most 1 to any group. For every index of mem, one group receives exactly 8 segments from the devices of that index, and no group receives more.
All inputs are finite; a program needn't handle non-finite values.
Results may differ from the reference program's by a relative error of at most 0.0075.
Values may be sent and summed in bfloat16 or wider, within the bound.
A program may use at most 128 MiB of HBM per device.

```python
import jax
import jax.numpy as jnp
from jax import lax

MELS = 80
CH = 1024
SCALE = 8
BR = 128
KERN0 = 5
BRANCH_DILATION = 2
SE_DIM = 128
ATT = 128
EMB = 192
LANGS = 107
FRAMES = 200
STORE = 8
N_GRP = 8
N_MEM = 4


def permute_row(row_key, row_values):
    return jax.random.permutation(row_key, row_values)


def draw_destination(key, part):
    groups = N_GRP
    extra = min(STORE, groups - STORE)

    def one_member(member):
        member_key = jax.random.fold_in(key, member)
        ranking = jax.random.permutation(jax.random.fold_in(member_key, 1), groups)
        source = jnp.arange(groups, dtype=jnp.int32)[:, None]
        column = jnp.arange(STORE, dtype=jnp.int32)[None, :]
        picked = (source + column) % groups
        special = (column == STORE - 1) & (source >= 1) & (source <= extra)
        picked = jnp.where(special, 0, picked)
        placed = ranking[picked]
        row_keys = jax.random.split(jax.random.fold_in(member_key, 2), groups)
        placed = jax.vmap(permute_row)(row_keys, placed)
        relabel = jax.random.permutation(jax.random.fold_in(member_key, 3), groups)
        return placed[relabel]
    tables = jax.vmap(one_member)(jnp.arange(N_MEM, dtype=jnp.int32))
    return jnp.transpose(tables, (1, 0, 2)).reshape(groups, N_MEM * STORE).astype(jnp.int32)


def steps_of(key, extent, cuts, least, largest):
    gain = 1.0
    for position, parts in cuts:
        draws = jax.random.uniform(jax.random.fold_in(jax.random.fold_in(key, 6), position), (parts,), jnp.float32, least / len(cuts), largest / len(cuts))
        gain = gain * jnp.repeat(jnp.exp(draws), extent[position] // parts).reshape((-1,) + (1,) * (len(extent) - 1 - position))
    return gain


def noise(key, shape, deviation, limit, shards=(), kind=jnp.bfloat16):
    array = deviation * jax.random.normal(key, shape, jnp.float32)
    if shards:
        array = array * steps_of(key, shape, shards, -0.22, 0.18)
    return jnp.clip(array, -limit, limit).astype(kind)


def setup_inputs(seed: int = 0) -> dict:
    splits = jax.random.split(jax.random.key(seed), 13)
    return {
        "filterbank": noise(splits[0], (N_GRP, N_MEM, STORE, FRAMES * MELS), 1.0, 6.0, ((0, 8), (1, 4)), jnp.float32),
        "destination": draw_destination(jax.random.fold_in(splits[12], 71), 0),
        "initial_conv_weight": noise(splits[2], (KERN0 * MELS, CH), (KERN0 * MELS) ** -0.5, 0.3125),
        "expand_weight": noise(splits[3], (CH, CH), CH ** -0.5, 0.1875),
        "branch_weight": noise(splits[4], (SCALE - 1, 3 * BR, BR), (3 * BR) ** -0.5, 0.3125),
        "merge_weight": noise(splits[5], (CH, CH), CH ** -0.5, 0.1875),
        "squeeze_weight": noise(splits[6], (CH, SE_DIM), CH ** -0.5, 0.1875),
        "excite_weight": noise(splits[7], (SE_DIM, CH), SE_DIM ** -0.5, 0.5),
        "attend_weight": noise(splits[8], (N_GRP, 3 * CH, ATT), CH ** -0.5, 0.1875, ((0, 8),)),
        "score_weight": noise(splits[9], (N_GRP, ATT, CH), ATT ** -0.5, 0.5, ((0, 8),)),
        "embed_weight": noise(splits[10], (N_GRP, 2 * CH, EMB), (2 * CH) ** -0.5, 0.125, ((0, 8),)),
        "language_weight": noise(splits[11], (N_GRP, EMB, LANGS), EMB ** -0.5, 0.4375, ((0, 8),)),
    }


EPS_STAT = 1e-05
EPS_NORM = 1e-06

def offset_frames(values, radius, spacing):
    frames = values.shape[1]
    padded = jnp.pad(values, ((0, 0), (radius * spacing, radius * spacing), (0, 0)))
    return jnp.concatenate([padded[:, offset * spacing:offset * spacing + frames] for offset in range(2 * radius + 1)], axis=2)

def trunk(features, initial_conv_weight, expand_weight, branch_weight, merge_weight, squeeze_weight, excite_weight):
    lowered = features.astype(jnp.bfloat16)
    columns = offset_frames(lowered, 2, 1)
    front_out = jax.nn.relu(jnp.einsum('nfk,kc->nfc', columns, initial_conv_weight, preferred_element_type=jnp.float32)).astype(jnp.bfloat16)
    expanded = jax.nn.relu(jnp.einsum('nfk,kc->nfc', front_out, expand_weight, preferred_element_type=jnp.float32)).astype(jnp.bfloat16)
    branch_width = expanded.shape[2] // SCALE
    pieces = [expanded[:, :, :branch_width]]
    previous = expanded[:, :, :branch_width]
    for branch in range(1, SCALE):
        present_frames = expanded[:, :, branch * branch_width:(branch + 1) * branch_width]
        if branch > 1:
            present_frames = (present_frames.astype(jnp.float32) + previous.astype(jnp.float32)).astype(jnp.bfloat16)
        stacked_rows = offset_frames(present_frames, 1, BRANCH_DILATION)
        previous = jax.nn.relu(jnp.einsum('nfk,kc->nfc', stacked_rows, branch_weight[branch - 1], preferred_element_type=jnp.float32)).astype(jnp.bfloat16)
        pieces.append(previous)
    joined = jnp.concatenate(pieces, axis=2)
    merged = jax.nn.relu(jnp.einsum('nfk,kc->nfc', joined, merge_weight, preferred_element_type=jnp.float32))
    squeezed = lax.optimization_barrier(jnp.mean(merged, axis=1))
    hidden = jax.nn.relu(jnp.dot(squeezed, squeeze_weight.astype(jnp.float32), precision=lax.Precision.HIGHEST))
    excited = jax.nn.sigmoid(jnp.dot(hidden, excite_weight.astype(jnp.float32), precision=lax.Precision.HIGHEST))
    return (front_out.astype(jnp.float32) + merged * excited[:, None, :]).astype(jnp.bfloat16)

def head(trunk_out, attend_weight, score_weight, embed_weight, language_weight):
    channels = trunk_out.shape[1]
    widened = trunk_out.astype(jnp.float32)
    center = lax.optimization_barrier(jnp.mean(widened, axis=0))
    spread = jnp.sqrt(lax.optimization_barrier(jnp.mean(jnp.square(widened - center), axis=0)) + EPS_STAT)
    context = jnp.dot(center, attend_weight[channels:2 * channels].astype(jnp.float32), precision=lax.Precision.HIGHEST)
    context = context + jnp.dot(spread, attend_weight[2 * channels:].astype(jnp.float32), precision=lax.Precision.HIGHEST)
    attended = jnp.tanh(jnp.dot(trunk_out, attend_weight[:channels], preferred_element_type=jnp.float32) + context).astype(jnp.bfloat16)
    signal_energy = jnp.dot(attended, score_weight, preferred_element_type=jnp.float32)
    weights = jnp.exp(signal_energy)
    weights = weights / lax.optimization_barrier(jnp.sum(weights, axis=0))
    pooled_mean = lax.optimization_barrier(jnp.sum(weights * widened, axis=0))
    pooled_std = jnp.sqrt(lax.optimization_barrier(jnp.sum(weights * jnp.square(widened - pooled_mean), axis=0)) + EPS_STAT)
    pooled_features = jnp.concatenate([pooled_mean, pooled_std]).astype(jnp.bfloat16)
    embedding = jnp.dot(pooled_features, embed_weight, preferred_element_type=jnp.float32)
    logits = jnp.dot(embedding.astype(jnp.bfloat16), language_weight, preferred_element_type=jnp.float32)
    return (embedding, logits)

def reference(filterbank, destination, initial_conv_weight, expand_weight, branch_weight, merge_weight, squeeze_weight, excite_weight, attend_weight, score_weight, embed_weight, language_weight):
    segments = filterbank.reshape(-1, FRAMES, MELS)
    targets = destination.reshape(-1).astype(jnp.int32)

    def score_one(segment):
        features, target = segment
        trunk_out = trunk(features[None], initial_conv_weight, expand_weight, branch_weight, merge_weight, squeeze_weight, excite_weight)[0]
        return head(trunk_out, attend_weight[target], score_weight[target], embed_weight[target], language_weight[target])
    embedding, logits = lax.map(score_one, (segments, targets))
    normed = (embedding * lax.rsqrt(lax.optimization_barrier(jnp.mean(jnp.square(embedding), axis=1, keepdims=True)) + EPS_NORM)).astype(jnp.bfloat16)
    normed = normed.reshape(N_GRP, N_MEM * STORE, EMB).astype(jnp.float32)
    similarity = jnp.einsum('gie,gje->gij', normed, normed, precision=lax.Precision.HIGHEST) / EMB
    return (logits.reshape(N_GRP, N_MEM * STORE, LANGS), similarity)
```

```python
import functools

import jax
import jax.numpy as jnp
from jax import lax
from jax.experimental import pallas as pl
from jax.experimental.pallas import tpu as pltpu
from jax.sharding import PartitionSpec as P

MELS = 80
SCALE = 8
FRAMES = 200
LANES = 128
FLAT_ROWS = 125
SEND_ROWS = 128
LEAD = 8
SLOT_ROWS = LEAD + SEND_ROWS
TAPS0 = 5
WINDOW = 512
TILE = 400
EPS_STAT = 1e-05
EPS_NORM = 1e-06

MESH = pl.DeviceIdType.MESH
F32 = jnp.float32
BF16 = jnp.bfloat16


def dot(a, b):
    return jnp.dot(a, b, preferred_element_type=F32)


def dot_split(values, weight):
    rows = values.shape[0]
    high = values.astype(BF16).astype(F32)
    both = jnp.concatenate([high, values - high], axis=0).astype(BF16)
    product = dot(both, weight)
    return product[:rows] + product[rows:]


def kernel(
    groups,
    members,
    bank_hbm,
    dest_ref,
    w0_hbm,
    expand_hbm,
    branch_hbm,
    merge_hbm,
    squeeze_hbm,
    excite_hbm,
    attend_hbm,
    score_hbm,
    embed_hbm,
    lang_hbm,
    logits_ref,
    sim_ref,
    bank,
    w0,
    expand,
    branch,
    merge,
    squeeze,
    excite,
    attend,
    score,
    embed,
    lang,
    staged,
    outbox,
    arrived,
    slots,
    cols,
    front,
    work,
    wide,
    ping,
    pong,
    attn,
    back,
    home,
    own,
    normed,
    gathered,
    load_sem,
    out_send,
    out_recv,
    back_send,
    back_recv,
    mem_send,
    mem_recv,
):
    stored = bank.shape[0]
    rows_all = FRAMES * groups
    tiles = rows_all // TILE
    tile_frames = TILE // groups
    channels = front.shape[1]
    me = lax.axis_index("grp")
    my_mem = lax.axis_index("mem")

    pairs = [
        (bank_hbm, bank),
        (w0_hbm, w0.at[pl.ds(0, w0_hbm.shape[0])]),
        (expand_hbm, expand),
        (branch_hbm, branch),
        (merge_hbm, merge),
        (squeeze_hbm, squeeze),
        (excite_hbm, excite),
        (attend_hbm, attend),
        (score_hbm, score),
        (embed_hbm, embed),
        (lang_hbm, lang),
    ]
    loads = [
        pltpu.make_async_copy(source, target, load_sem.at[i])
        for i, (source, target) in enumerate(pairs)
    ]
    for load in loads:
        load.start()

    barrier = pltpu.get_barrier_semaphore()
    for step in range(1, groups):
        pl.semaphore_signal(
            barrier, inc=1, device_id=(lax.rem(me + step, groups), my_mem), device_id_type=MESH
        )
    for step in range(1, members):
        pl.semaphore_signal(
            barrier, inc=1, device_id=(me, lax.rem(my_mem + step, members)), device_id_type=MESH
        )

    staged[...] = jnp.zeros_like(staged)
    slots[...] = jnp.zeros_like(slots)
    w0[w0_hbm.shape[0] :, :] = jnp.zeros((WINDOW - w0_hbm.shape[0], channels), BF16)
    halo = 2 * groups
    for buffer in (ping, pong):
        buffer[:halo, :] = jnp.zeros((halo, LANES), BF16)
        buffer[halo + rows_all :, :] = jnp.zeros((halo, LANES), BF16)
    back[...] = jnp.zeros_like(back)

    loads[0].wait()
    for row in range(FLAT_ROWS):
        staged[pl.ds(row, stored, stride=SEND_ROWS), :] = bank[:, row * LANES : (row + 1) * LANES]

    pl.semaphore_wait(barrier, groups - 1 + members - 1)

    def segment_for(group):
        picked = jnp.zeros((SEND_ROWS, LANES), F32)
        for s in range(stored):
            rows = staged[s * SEND_ROWS : (s + 1) * SEND_ROWS, :]
            picked = jnp.where(dest_ref[0, s] == group, rows, picked)
        return picked.astype(BF16)

    sends = []
    for step in range(1, groups):
        group = lax.rem(me + step, groups)
        outbox[step] = segment_for(group)
        copy = pltpu.make_async_remote_copy(
            src_ref=outbox.at[step],
            dst_ref=arrived.at[me],
            send_sem=out_send.at[step],
            recv_sem=out_recv.at[me],
            device_id=(group, my_mem),
            device_id_type=MESH,
        )
        copy.start()
        sends.append(copy)
    arrived[me] = segment_for(me)

    def place(slot):
        start = pl.multiple_of(slot * SLOT_ROWS + LEAD, 8)
        slots[pl.ds(start, SEND_ROWS), :] = arrived[slot].astype(F32)

    place(me)
    for step in range(1, groups):
        source = lax.rem(me + groups - step, groups)
        pltpu.make_async_remote_copy(
            src_ref=outbox.at[step],
            dst_ref=arrived.at[source],
            send_sem=out_send.at[step],
            recv_sem=out_recv.at[source],
            device_id=(source, my_mem),
            device_id_type=MESH,
        ).wait_recv()
        place(source)

    lane = lax.broadcasted_iota(jnp.int32, (groups, LANES), 1)

    def windows(block, _):
        first = block * 5
        held = {}

        def row_at(index):
            if index not in held:
                held[index] = slots[pl.ds(first + index, groups, stride=SLOT_ROWS), :]
            return held[index]

        pair = []
        for phase in range(8):
            begin = phase * MELS + LEAD * LANES - 2 * MELS
            index, offset = begin // LANES, begin % LANES
            pieces = []
            for j in range(4):
                low = row_at(index + j)
                if offset:
                    high = row_at(index + j + 1) if j < 3 else None
                    low = pltpu.roll(low, LANES - offset, 1)
                    if high is not None:
                        high = pltpu.roll(high, LANES - offset, 1)
                        low = jnp.where(lane < LANES - offset, low, high)
                if j == 3:
                    low = jnp.where(lane < TAPS0 * MELS - 3 * LANES, low, 0.0)
                pieces.append(low)
            pair.append(jnp.concatenate(pieces, axis=1))
            if len(pair) == 2:
                start = pl.multiple_of((block * 8 + phase - 1) * groups, 16)
                cols[pl.ds(start, 2 * groups), :] = jnp.concatenate(pair, axis=0).astype(BF16)
                pair = []
        return 0

    lax.fori_loop(0, FRAMES // 8, windows, 0)

    loads[1].wait()
    loads[2].wait()

    def first_layers(tile, _):
        start = pl.multiple_of(tile * TILE, 16)
        rows = pl.ds(start, TILE)
        out = jnp.maximum(dot(cols[rows, :], w0[...]), 0.0).astype(BF16)
        front[rows, :] = out
        expanded = jnp.maximum(dot(out, expand[...]), 0.0).astype(BF16)
        work[rows, :] = expanded
        ping[pl.ds(start + halo, TILE), :] = expanded[:, LANES : 2 * LANES]
        return 0

    lax.fori_loop(0, tiles, first_layers, 0)

    loads[3].wait()
    buffers = (ping, pong)
    for i in range(1, SCALE):
        source, target = buffers[(i - 1) % 2], buffers[i % 2]

        def one_branch(tile, _, i=i, source=source, target=target):
            start = pl.multiple_of(tile * 2 * TILE, 16)
            rows = pl.ds(start, 2 * TILE)
            stacked = jnp.concatenate(
                [source[pl.ds(start + k * halo, 2 * TILE), :] for k in range(3)], axis=1
            )
            out = jnp.maximum(dot(stacked, branch[i - 1]), 0.0).astype(BF16)
            work[rows, i * LANES : (i + 1) * LANES] = out
            if i < SCALE - 1:
                following = work[rows, (i + 1) * LANES : (i + 2) * LANES].astype(F32)
                target[pl.ds(start + halo, 2 * TILE), :] = (following + out.astype(F32)).astype(BF16)
            return 0

        lax.fori_loop(0, tiles // 2, one_branch, 0, unroll=True)

    loads[4].wait()

    def by_frame(values):
        return values.reshape(tile_frames, groups, values.shape[1])

    def merging(tile, total):
        rows = pl.ds(pl.multiple_of(tile * TILE, 16), TILE)
        merged = jnp.maximum(dot(work[rows, :], merge[...]), 0.0)
        wide[rows, :] = merged
        return total + jnp.sum(by_frame(merged), axis=0)

    zeros = jnp.zeros((groups, channels), F32)
    total = lax.fori_loop(0, tiles, merging, zeros)

    loads[5].wait()
    loads[6].wait()
    hidden = jnp.maximum(dot_split(total / FRAMES, squeeze[...]), 0.0)
    excited = 1.0 / (1.0 + jnp.exp(-dot_split(hidden, excite[...])))

    loads[7].wait()
    pivot = front[0 : 2 * groups, :].astype(F32)[:groups] + wide[0:groups, :] * excited

    def trunk_out(tile, carry):
        first, second = carry
        rows = pl.ds(pl.multiple_of(tile * TILE, 16), TILE)
        out = by_frame(front[rows, :].astype(F32)) + by_frame(wide[rows, :]) * excited
        out = out.reshape(TILE, channels).astype(BF16)
        work[rows, :] = out
        attn[rows, :] = dot(out, attend[0:channels, :])
        moved = by_frame(out.astype(F32)) - pivot
        return first + jnp.sum(moved, axis=0), second + jnp.sum(moved * moved, axis=0)

    first, second = lax.fori_loop(0, tiles, trunk_out, (zeros, zeros))
    shift = first / FRAMES
    center = pivot + shift
    spread = jnp.sqrt(jnp.maximum(second / FRAMES - shift * shift, 0.0) + EPS_STAT)
    context = dot_split(center, attend[channels : 2 * channels, :]) + dot_split(
        spread, attend[2 * channels :, :]
    )

    loads[8].wait()

    def energies(tile, total):
        rows = pl.ds(pl.multiple_of(tile * TILE, 16), TILE)
        attended = jnp.tanh(by_frame(attn[rows, :]) + context).reshape(TILE, -1).astype(BF16)
        weights = jnp.exp(dot(attended, score[...]))
        wide[rows, :] = weights
        return total + jnp.sum(by_frame(weights), axis=0)

    scale = 1.0 / lax.fori_loop(0, tiles, energies, zeros)

    def weighted(tile, total):
        rows = pl.ds(pl.multiple_of(tile * TILE, 16), TILE)
        weights = by_frame(wide[rows, :]) * scale
        return total + jnp.sum(weights * by_frame(work[rows, :].astype(F32)), axis=0)

    mean = lax.fori_loop(0, tiles, weighted, zeros)

    def deviating(tile, total):
        rows = pl.ds(pl.multiple_of(tile * TILE, 16), TILE)
        weights = by_frame(wide[rows, :]) * scale
        moved = by_frame(work[rows, :].astype(F32)) - mean
        return total + jnp.sum(weights * (moved * moved), axis=0)

    deviation = jnp.sqrt(lax.fori_loop(0, tiles, deviating, zeros) + EPS_STAT)

    loads[9].wait()
    loads[10].wait()
    pooled = jnp.concatenate([mean, deviation], axis=1).astype(BF16)
    embedding = dot(pooled, embed[...])
    scores = dot(embedding.astype(BF16), lang[...])
    width = embedding.shape[1]
    langs = scores.shape[1]
    back[:, 0, :] = embedding[:, :LANES]
    back[:, 1, : width - LANES] = embedding[:, LANES:]
    back[:, 2, :langs] = scores

    for step in range(1, groups):
        group = lax.rem(me + step, groups)
        copy = pltpu.make_async_remote_copy(
            src_ref=back.at[group],
            dst_ref=home.at[me],
            send_sem=back_send.at[step],
            recv_sem=back_recv.at[me],
            device_id=(group, my_mem),
            device_id_type=MESH,
        )
        copy.start()
        sends.append(copy)
    home[me] = back[me]
    for step in range(1, groups):
        source = lax.rem(me + groups - step, groups)
        pltpu.make_async_remote_copy(
            src_ref=back.at[source],
            dst_ref=home.at[source],
            send_sem=back_send.at[step],
            recv_sem=back_recv.at[source],
            device_id=(source, my_mem),
            device_id_type=MESH,
        ).wait_recv()
    for s in range(stored):
        picked = home[0]
        for group in range(1, groups):
            picked = jnp.where(dest_ref[0, s] == group, home[group], picked)
        own[s] = picked

    left, right = own[:, 0, :], own[:, 1, :]
    logits_ref[...] = own[:, 2, :][:, :langs]
    squares = jnp.sum(left * left + right * right, axis=1, keepdims=True)
    factor = lax.rsqrt(squares / width + EPS_NORM)
    mine = jnp.concatenate([left * factor, right * factor], axis=1).astype(BF16)
    normed[...] = mine.astype(F32)
    for step in range(1, members):
        member = lax.rem(my_mem + step, members)
        copy = pltpu.make_async_remote_copy(
            src_ref=normed,
            dst_ref=gathered.at[my_mem],
            send_sem=mem_send.at[step],
            recv_sem=mem_recv.at[my_mem],
            device_id=(me, member),
            device_id_type=MESH,
        )
        copy.start()
        sends.append(copy)
    gathered[my_mem] = normed[...]
    for step in range(1, members):
        source = lax.rem(my_mem + members - step, members)
        pltpu.make_async_remote_copy(
            src_ref=normed,
            dst_ref=gathered.at[source],
            send_sem=mem_send.at[step],
            recv_sem=mem_recv.at[source],
            device_id=(me, source),
            device_id_type=MESH,
        ).wait_recv()
    every = gathered[...].reshape(members * stored, 2 * LANES).astype(BF16)
    sim_ref[...] = (
        lax.dot_general(mine, every, (((1,), (1,)), ((), ())), preferred_element_type=F32) / width
    )
    for copy in sends:
        copy.wait_send()


def shards(
    filterbank,
    destination,
    initial_conv_weight,
    expand_weight,
    branch_weight,
    merge_weight,
    squeeze_weight,
    excite_weight,
    attend_weight,
    score_weight,
    embed_weight,
    language_weight,
):
    groups = lax.axis_size("grp")
    members = lax.axis_size("mem")
    stored = filterbank.shape[2]
    rows = FRAMES * groups
    channels = expand_weight.shape[0]
    langs = language_weight.shape[2]
    operands = (
        filterbank.reshape(stored, FRAMES * MELS),
        destination,
        initial_conv_weight,
        expand_weight,
        branch_weight,
        merge_weight,
        squeeze_weight,
        excite_weight,
        attend_weight[0],
        score_weight[0],
        embed_weight[0],
        language_weight[0],
    )
    copied = [pltpu.VMEM(a.shape, a.dtype) for a in operands]
    del copied[1]
    copied[1] = pltpu.VMEM((WINDOW, channels), BF16)
    anywhere = pl.BlockSpec(memory_space=pl.ANY)
    in_specs = [anywhere] * len(operands)
    in_specs[1] = pl.BlockSpec(memory_space=pltpu.SMEM)
    dma = pltpu.SemaphoreType.DMA
    logits, similarity = pl.pallas_call(
        functools.partial(kernel, groups, members),
        out_shape=(
            jax.ShapeDtypeStruct((stored, langs), F32),
            jax.ShapeDtypeStruct((stored, members * stored), F32),
        ),
        in_specs=in_specs,
        out_specs=[pl.BlockSpec(memory_space=pltpu.VMEM)] * 2,
        scratch_shapes=copied
        + [
            pltpu.VMEM((stored * SEND_ROWS, LANES), F32),
            pltpu.VMEM((groups, SEND_ROWS, LANES), BF16),
            pltpu.VMEM((groups, SEND_ROWS, LANES), BF16),
            pltpu.VMEM((groups * SLOT_ROWS, LANES), F32),
            pltpu.VMEM((rows, WINDOW), BF16),
            pltpu.VMEM((rows, channels), BF16),
            pltpu.VMEM((rows, channels), BF16),
            pltpu.VMEM((rows, channels), F32),
            pltpu.VMEM((rows + 4 * groups, LANES), BF16),
            pltpu.VMEM((rows + 4 * groups, LANES), BF16),
            pltpu.VMEM((rows, LANES), F32),
            pltpu.VMEM((groups, 8, LANES), F32),
            pltpu.VMEM((groups, 8, LANES), F32),
            pltpu.VMEM((stored, 8, LANES), F32),
            pltpu.VMEM((stored, 2 * LANES), F32),
            pltpu.VMEM((members, stored, 2 * LANES), F32),
            dma((len(copied),)),
            dma((groups,)),
            dma((groups,)),
            dma((groups,)),
            dma((groups,)),
            dma((members,)),
            dma((members,)),
        ],
        compiler_params=pltpu.CompilerParams(
            collective_id=0, has_side_effects=True, vmem_limit_bytes=60 * 1024 * 1024
        ),
        cost_estimate=pl.CostEstimate(
            flops=rows * 12_000_000, bytes_accessed=10_000_000, transcendentals=rows * 1200
        ),
    )(*operands)
    return (logits[None], similarity[None])


def solution(mesh):
    return jax.shard_map(
        shards,
        mesh=mesh,
        in_specs=(
            P("grp", "mem", None, None),
            P("grp", "mem"),
            P(),
            P(),
            P(),
            P(),
            P(),
            P(),
            P("grp", None, None),
            P("grp", None, None),
            P("grp", None, None),
            P("grp", None, None),
        ),
        out_specs=(P("grp", "mem", None), P("grp", "mem", None)),
        check_vma=False,
    )
```

```python
import functools

import jax
import jax.numpy as jnp
from jax import lax
from jax.experimental import pallas as pl
from jax.experimental.pallas import tpu as pltpu
from jax.sharding import PartitionSpec as P

MELS = 80
SCALE = 8
FRAMES = 200
LANES = 128
FLAT_ROWS = 125
SEND_ROWS = 128
LEAD = 8
SLOT_ROWS = LEAD + SEND_ROWS
TAPS0 = 5
WINDOW = 512
TILE = 400
CHUNK = 256
EPS_STAT = 1e-05
EPS_NORM = 1e-06

MESH = pl.DeviceIdType.MESH
F32 = jnp.float32
BF16 = jnp.bfloat16


def dot(a, b):
    return jnp.dot(a, b, preferred_element_type=F32)


def dot_split(values, weight):
    rows = values.shape[0]
    high = values.astype(BF16).astype(F32)
    both = jnp.concatenate([high, values - high], axis=0).astype(BF16)
    product = dot(both, weight)
    return product[:rows] + product[rows:]


def kernel(
    groups,
    members,
    bank_hbm,
    dest_ref,
    w0_hbm,
    expand_hbm,
    branch_hbm,
    merge_hbm,
    squeeze_hbm,
    excite_hbm,
    attend_hbm,
    score_hbm,
    embed_hbm,
    lang_hbm,
    result_ref,
    bank,
    w0,
    expand,
    branch,
    merge,
    squeeze,
    excite,
    attend,
    score,
    embed,
    lang,
    staged,
    outbox,
    arrived,
    slots,
    cols,
    front,
    work,
    wide,
    ping,
    pong,
    attn,
    back,
    home,
    own,
    normed,
    gathered,
    load_sem,
    out_send,
    out_recv,
    back_send,
    back_recv,
    mem_send,
    mem_recv,
):
    stored = bank.shape[0]
    rows_all = FRAMES * groups
    tiles = rows_all // TILE
    tile_frames = TILE // groups
    channels = front.shape[1]
    me = lax.axis_index("grp")
    my_mem = lax.axis_index("mem")

    pairs = [
        (bank_hbm, bank),
        (w0_hbm, w0.at[pl.ds(0, w0_hbm.shape[0])]),
        (expand_hbm, expand),
        (branch_hbm, branch.at[:, pl.ds(0, 3 * LANES), pl.ds(0, LANES)]),
        (branch_hbm, branch.at[:, pl.ds(LANES, 3 * LANES), pl.ds(LANES, LANES)]),
        (merge_hbm, merge),
        (squeeze_hbm, squeeze),
        (excite_hbm, excite),
        (attend_hbm, attend),
        (score_hbm, score),
        (embed_hbm, embed),
        (lang_hbm, lang),
    ]
    loads = [
        pltpu.make_async_copy(source, target, load_sem.at[i])
        for i, (source, target) in enumerate(pairs)
    ]
    for load in loads:
        load.start()

    barrier = pltpu.get_barrier_semaphore()
    for step in range(1, groups):
        pl.semaphore_signal(
            barrier, inc=1, device_id=(lax.rem(me + step, groups), my_mem), device_id_type=MESH
        )
    for step in range(1, members):
        pl.semaphore_signal(
            barrier, inc=1, device_id=(me, lax.rem(my_mem + step, members)), device_id_type=MESH
        )

    staged[...] = jnp.zeros_like(staged)
    slots[...] = jnp.zeros_like(slots)
    w0[w0_hbm.shape[0] :, :] = jnp.zeros((WINDOW - w0_hbm.shape[0], channels), BF16)
    halo = 2 * groups
    half = rows_all // 2
    for buffer in (ping, pong):
        buffer[0, half:, :] = jnp.zeros((halo, LANES), BF16)
        buffer[1, :halo, :] = jnp.zeros((halo, LANES), BF16)
    empty = jnp.zeros((SCALE - 1, LANES, LANES), BF16)
    branch[:, 3 * LANES :, :LANES] = empty
    branch[:, :LANES, LANES:] = empty
    back[...] = jnp.zeros_like(back)

    loads[0].wait()
    for row in range(FLAT_ROWS):
        staged[pl.ds(row, stored, stride=SEND_ROWS), :] = bank[:, row * LANES : (row + 1) * LANES]

    def segment_for(group):
        picked = jnp.zeros((SEND_ROWS, LANES), F32)
        for s in range(stored):
            rows = staged[s * SEND_ROWS : (s + 1) * SEND_ROWS, :]
            picked = jnp.where(dest_ref[0, s] == group, rows, picked)
        return picked.astype(BF16)

    for step in range(1, groups):
        outbox[step] = segment_for(lax.rem(me + step, groups))

    pl.semaphore_wait(barrier, groups - 1 + members - 1)

    sends = []
    for step in range(1, groups):
        group = lax.rem(me + step, groups)
        copy = pltpu.make_async_remote_copy(
            src_ref=outbox.at[step],
            dst_ref=arrived.at[me],
            send_sem=out_send.at[step],
            recv_sem=out_recv.at[me],
            device_id=(group, my_mem),
            device_id_type=MESH,
        )
        copy.start()
        sends.append(copy)
    arrived[me] = segment_for(me)

    def place(slot):
        start = pl.multiple_of(slot * SLOT_ROWS + LEAD, 8)
        slots[pl.ds(start, SEND_ROWS), :] = arrived[slot].astype(F32)

    place(me)
    for step in range(1, groups):
        source = lax.rem(me + groups - step, groups)
        pltpu.make_async_remote_copy(
            src_ref=outbox.at[step],
            dst_ref=arrived.at[source],
            send_sem=out_send.at[step],
            recv_sem=out_recv.at[source],
            device_id=(source, my_mem),
            device_id_type=MESH,
        ).wait_recv()
        place(source)

    lane = lax.broadcasted_iota(jnp.int32, (groups, LANES), 1)

    def windows(block, _):
        first = block * 5
        held = {}

        def row_at(index):
            if index not in held:
                held[index] = slots[pl.ds(first + index, groups, stride=SLOT_ROWS), :]
            return held[index]

        pair = []
        for phase in range(8):
            begin = phase * MELS + LEAD * LANES - 2 * MELS
            index, offset = begin // LANES, begin % LANES
            pieces = []
            for j in range(4):
                low = row_at(index + j)
                if offset:
                    high = row_at(index + j + 1) if j < 3 else None
                    low = pltpu.roll(low, LANES - offset, 1)
                    if high is not None:
                        high = pltpu.roll(high, LANES - offset, 1)
                        low = jnp.where(lane < LANES - offset, low, high)
                if j == 3:
                    low = jnp.where(lane < TAPS0 * MELS - 3 * LANES, low, 0.0)
                pieces.append(low)
            pair.append(jnp.concatenate(pieces, axis=1))
            if len(pair) == 2:
                side, place_in = phase // 2 % 2, phase // 4
                start = pl.multiple_of(side * half + (block * 2 + place_in) * halo, 16)
                cols[pl.ds(start, 2 * groups), :] = jnp.concatenate(pair, axis=0).astype(BF16)
                pair = []
        return 0

    lax.fori_loop(0, FRAMES // 8, windows, 0)

    loads[1].wait()
    loads[2].wait()

    chunks = [slice(c, c + CHUNK) for c in range(0, channels, CHUNK)]
    half_tiles = tiles // 2

    def first_layers(tile, _):
        rows = pl.ds(pl.multiple_of(tile * TILE, 16), TILE)
        for chunk in chunks:
            out = jnp.maximum(dot(cols[rows, :], w0[:, chunk]), 0.0)
            front[rows, chunk] = out.astype(BF16)
        side = tile // half_tiles
        start = pl.multiple_of(tile % half_tiles * TILE + side * halo, 16)
        for chunk in chunks:
            expanded = jnp.maximum(dot(front[rows, :], expand[:, chunk]), 0.0).astype(BF16)
            work[rows, chunk] = expanded
            if chunk.start == 0:
                ping[side, pl.ds(start, TILE), :] = expanded[:, LANES : 2 * LANES]
        return 0

    lax.fori_loop(0, tiles, first_layers, 0)

    loads[3].wait()
    loads[4].wait()
    buffers = (ping, pong)
    for i in range(1, SCALE):
        source, target = buffers[(i - 1) % 2], buffers[i % 2]

        def one_branch(tile, _, i=i, source=source, target=target):
            start = pl.multiple_of(tile * TILE, 16)
            near, far = pl.ds(start, TILE), pl.ds(start + halo, TILE)
            window = jnp.concatenate(
                [source[1, near, :], source[0, near, :], source[1, far, :], source[0, far, :]], axis=1
            )
            out = jnp.maximum(dot(window, branch[i - 1]), 0.0).astype(BF16)
            for side, spot in ((0, near), (1, far)):
                rows = pl.ds(start + side * half, TILE)
                mine = out[:, side * LANES : (side + 1) * LANES]
                work[rows, i * LANES : (i + 1) * LANES] = mine
                if i < SCALE - 1:
                    following = work[rows, (i + 1) * LANES : (i + 2) * LANES].astype(F32)
                    target[side, spot, :] = (following + mine.astype(F32)).astype(BF16)
            return 0

        lax.fori_loop(0, half_tiles, one_branch, 0, unroll=True)

    loads[5].wait()

    def by_frame(values):
        return values.reshape(tile_frames, groups, values.shape[1])

    def merging(tile, total):
        rows = pl.ds(pl.multiple_of(tile * TILE, 16), TILE)
        sums = []
        for chunk in chunks:
            merged = jnp.maximum(dot(work[rows, :], merge[:, chunk]), 0.0)
            wide[rows, chunk] = merged
            sums.append(jnp.sum(by_frame(merged), axis=0))
        return total + jnp.concatenate(sums, axis=1)

    zeros = jnp.zeros((groups, channels), F32)
    total = lax.fori_loop(0, tiles, merging, zeros)

    loads[6].wait()
    loads[7].wait()
    hidden = jnp.maximum(dot_split(total / FRAMES, squeeze[...]), 0.0)
    excited = 1.0 / (1.0 + jnp.exp(-dot_split(hidden, excite[...])))

    loads[8].wait()
    pivot = front[0 : 2 * groups, :].astype(F32)[:groups] + wide[0:groups, :] * excited

    def trunk_out(tile, carry):
        first, second = carry
        rows = pl.ds(pl.multiple_of(tile * TILE, 16), TILE)
        sums, squares = [], []
        for chunk in chunks:
            out = by_frame(wide[rows, chunk]) * excited[:, chunk]
            out = by_frame(front[rows, chunk].astype(F32)) + out
            out = out.reshape(TILE, CHUNK).astype(BF16)
            work[rows, chunk] = out
            moved = by_frame(out.astype(F32)) - pivot[:, chunk]
            sums.append(jnp.sum(moved, axis=0))
            squares.append(jnp.sum(moved * moved, axis=0))
        attn[rows, :] = dot(work[rows, :], attend[0:channels, :])
        return first + jnp.concatenate(sums, axis=1), second + jnp.concatenate(squares, axis=1)

    first, second = lax.fori_loop(0, tiles, trunk_out, (zeros, zeros))
    shift = first / FRAMES
    center = pivot + shift
    spread = jnp.sqrt(jnp.maximum(second / FRAMES - shift * shift, 0.0) + EPS_STAT)
    context = dot_split(center, attend[channels : 2 * channels, :]) + dot_split(
        spread, attend[2 * channels :, :]
    )

    loads[9].wait()

    inverse = 1.0 / spread

    def energies(tile, carry):
        rows = pl.ds(pl.multiple_of(tile * TILE, 16), TILE)
        attended = jnp.tanh(by_frame(attn[rows, :]) + context).reshape(TILE, -1).astype(BF16)
        parts = ([], [], [])
        for chunk in chunks:
            weights = by_frame(jnp.exp(dot(attended, score[:, chunk])))
            value = by_frame(work[rows, chunk].astype(F32))
            value = (value - center[:, chunk]) * inverse[:, chunk]
            parts[0].append(jnp.sum(weights, axis=0))
            weights = weights * value
            parts[1].append(jnp.sum(weights, axis=0))
            parts[2].append(jnp.sum(weights * value, axis=0))
        return tuple(c + jnp.concatenate(p, axis=1) for c, p in zip(carry, parts))

    norm, weighted, squared = lax.fori_loop(0, tiles, energies, (zeros, zeros, zeros))
    weighted = weighted / norm
    squared = jnp.maximum(squared / norm - weighted * weighted, 0.0)
    mean = center + spread * weighted
    deviation = jnp.sqrt(spread * spread * squared + EPS_STAT)

    loads[10].wait()
    loads[11].wait()
    pooled = jnp.concatenate([mean, deviation], axis=1).astype(BF16)
    embedding = lax.dot_general(
        pooled, embed[...], (((1,), (1,)), ((), ())), preferred_element_type=F32
    )
    scores = dot(embedding.astype(BF16), lang[...])
    width = embedding.shape[1]
    langs = scores.shape[1]
    back[:, 0, :] = embedding[:, :LANES]
    back[:, 1, : width - LANES] = embedding[:, LANES:]
    back[:, 2, :langs] = scores

    for step in range(1, groups):
        group = lax.rem(me + step, groups)
        copy = pltpu.make_async_remote_copy(
            src_ref=back.at[group],
            dst_ref=home.at[me],
            send_sem=back_send.at[step],
            recv_sem=back_recv.at[me],
            device_id=(group, my_mem),
            device_id_type=MESH,
        )
        copy.start()
        sends.append(copy)
    home[me] = back[me]
    for step in range(1, groups):
        source = lax.rem(me + groups - step, groups)
        pltpu.make_async_remote_copy(
            src_ref=back.at[source],
            dst_ref=home.at[source],
            send_sem=back_send.at[step],
            recv_sem=back_recv.at[source],
            device_id=(source, my_mem),
            device_id_type=MESH,
        ).wait_recv()
    for s in range(stored):
        picked = home[0]
        for group in range(1, groups):
            picked = jnp.where(dest_ref[0, s] == group, home[group], picked)
        own[s] = picked

    left, right = own[:, 0, :], own[:, 1, :]
    result_ref[:, :LANES] = own[:, 2, :]
    squares = jnp.sum(left * left + right * right, axis=1, keepdims=True)
    factor = lax.rsqrt(squares / width + EPS_NORM)
    mine = jnp.concatenate([left * factor, right * factor], axis=1).astype(BF16)
    normed[...] = mine.astype(F32)
    for step in range(1, members):
        member = lax.rem(my_mem + step, members)
        copy = pltpu.make_async_remote_copy(
            src_ref=normed,
            dst_ref=gathered.at[my_mem],
            send_sem=mem_send.at[step],
            recv_sem=mem_recv.at[my_mem],
            device_id=(me, member),
            device_id_type=MESH,
        )
        copy.start()
        sends.append(copy)
    gathered[my_mem] = normed[...]
    for step in range(1, members):
        source = lax.rem(my_mem + members - step, members)
        pltpu.make_async_remote_copy(
            src_ref=normed,
            dst_ref=gathered.at[source],
            send_sem=mem_send.at[step],
            recv_sem=mem_recv.at[source],
            device_id=(me, source),
            device_id_type=MESH,
        ).wait_recv()
    every = gathered[...].reshape(members * stored, 2 * LANES).astype(BF16)
    inner = lax.dot_general(mine, every, (((1,), (1,)), ((), ())), preferred_element_type=F32)
    result_ref[:, LANES : LANES + members * stored] = inner / width
    for copy in sends:
        copy.wait_send()


def split_result(result_ref, logits_ref, sim_ref):
    logits_ref[0] = result_ref[:, : logits_ref.shape[2]]
    sim_ref[0] = result_ref[:, LANES : LANES + sim_ref.shape[2]]


def shards(
    filterbank,
    destination,
    initial_conv_weight,
    expand_weight,
    branch_weight,
    merge_weight,
    squeeze_weight,
    excite_weight,
    attend_weight,
    score_weight,
    embed_weight,
    language_weight,
):
    groups = lax.axis_size("grp")
    members = lax.axis_size("mem")
    stored = filterbank.shape[2]
    rows = FRAMES * groups
    channels = expand_weight.shape[0]
    langs = language_weight.shape[2]
    operands = (
        filterbank.reshape(stored, FRAMES * MELS),
        destination,
        initial_conv_weight,
        expand_weight,
        branch_weight,
        merge_weight,
        squeeze_weight,
        excite_weight,
        attend_weight[0],
        score_weight[0],
        embed_weight[0].T,
        language_weight[0],
    )
    copied = [pltpu.VMEM(a.shape, a.dtype) for a in operands]
    del copied[1]
    copied[1] = pltpu.VMEM((WINDOW, channels), BF16)
    copied[3] = pltpu.VMEM((SCALE - 1, 4 * LANES, 2 * LANES), BF16)
    anywhere = pl.BlockSpec(memory_space=pl.ANY)
    in_specs = [anywhere] * len(operands)
    in_specs[1] = pl.BlockSpec(memory_space=pltpu.SMEM)
    dma = pltpu.SemaphoreType.DMA
    result = pl.pallas_call(
        functools.partial(kernel, groups, members),
        out_shape=jax.ShapeDtypeStruct((stored, 2 * LANES), F32),
        in_specs=in_specs,
        out_specs=pl.BlockSpec(memory_space=pltpu.VMEM),
        scratch_shapes=copied
        + [
            pltpu.VMEM((stored * SEND_ROWS, LANES), F32),
            pltpu.VMEM((groups, SEND_ROWS, LANES), BF16),
            pltpu.VMEM((groups, SEND_ROWS, LANES), BF16),
            pltpu.VMEM((groups * SLOT_ROWS, LANES), F32),
            pltpu.VMEM((rows, WINDOW), BF16),
            pltpu.VMEM((rows, channels), BF16),
            pltpu.VMEM((rows, channels), BF16),
            pltpu.VMEM((rows, channels), F32),
            pltpu.VMEM((2, rows // 2 + 2 * groups, LANES), BF16),
            pltpu.VMEM((2, rows // 2 + 2 * groups, LANES), BF16),
            pltpu.VMEM((rows, LANES), F32),
            pltpu.VMEM((groups, 8, LANES), F32),
            pltpu.VMEM((groups, 8, LANES), F32),
            pltpu.VMEM((stored, 8, LANES), F32),
            pltpu.VMEM((stored, 2 * LANES), F32),
            pltpu.VMEM((members, stored, 2 * LANES), F32),
            dma((len(copied) + 1,)),
            dma((groups,)),
            dma((groups,)),
            dma((groups,)),
            dma((groups,)),
            dma((members,)),
            dma((members,)),
        ],
        compiler_params=pltpu.CompilerParams(
            collective_id=0, has_side_effects=True, vmem_limit_bytes=60 * 1024 * 1024
        ),
        cost_estimate=pl.CostEstimate(
            flops=rows * 12_000_000, bytes_accessed=10_000_000, transcendentals=rows * 1200
        ),
    )(*operands)
    return pl.pallas_call(
        split_result,
        out_shape=(
            jax.ShapeDtypeStruct((1, stored, langs), F32),
            jax.ShapeDtypeStruct((1, stored, members * stored), F32),
        ),
    )(result)


def solution(mesh):
    return jax.shard_map(
        shards,
        mesh=mesh,
        in_specs=(
            P("grp", "mem", None, None),
            P("grp", "mem"),
            P(),
            P(),
            P(),
            P(),
            P(),
            P(),
            P("grp", None, None),
            P("grp", None, None),
            P("grp", None, None),
            P("grp", None, None),
        ),
        out_specs=(P("grp", "mem", None), P("grp", "mem", None)),
        check_vma=False,
    )
```

```python
import functools

import jax
import jax.numpy as jnp
from jax import lax
from jax.experimental import pallas as pl
from jax.experimental.pallas import tpu as pltpu
from jax.sharding import PartitionSpec as P

MELS = 80
SCALE = 8
FRAMES = 200
LANES = 128
FLAT_ROWS = 125
SEND_ROWS = 128
LEAD = 8
SLOT_ROWS = LEAD + SEND_ROWS
TAPS0 = 5
WINDOW = 512
TILE = 400
TALL = 800
CHUNK = 256
EPS_STAT = 1e-05
EPS_NORM = 1e-06

MESH = pl.DeviceIdType.MESH
F32 = jnp.float32
BF16 = jnp.bfloat16


def dot(a, b):
    return jnp.dot(a, b, preferred_element_type=F32)


def dot_split(values, weight):
    rows = values.shape[0]
    high = values.astype(BF16).astype(F32)
    both = jnp.concatenate([high, values - high], axis=0).astype(BF16)
    product = dot(both, weight)
    return product[:rows] + product[rows:]


def kernel(
    groups,
    members,
    bank_hbm,
    dest_ref,
    w0_hbm,
    expand_hbm,
    branch_hbm,
    merge_hbm,
    squeeze_hbm,
    excite_hbm,
    attend_hbm,
    score_hbm,
    embed_hbm,
    lang_hbm,
    result_ref,
    bank,
    w0,
    expand,
    branch,
    merge,
    squeeze,
    excite,
    attend,
    score,
    embed,
    lang,
    staged,
    outbox,
    arrived,
    slots,
    cols,
    front,
    work,
    wide,
    ping,
    pong,
    attn,
    back,
    home,
    own,
    normed,
    gathered,
    load_sem,
    out_send,
    out_recv,
    back_send,
    back_recv,
    mem_send,
    mem_recv,
):
    stored = bank.shape[0]
    rows_all = FRAMES * groups
    tiles = rows_all // TILE
    talls = rows_all // TALL
    channels = front.shape[1]
    me = lax.axis_index("grp")
    my_mem = lax.axis_index("mem")

    pairs = [
        (bank_hbm, bank),
        (w0_hbm, w0.at[pl.ds(0, w0_hbm.shape[0])]),
        (expand_hbm, expand),
        (branch_hbm, branch.at[:, pl.ds(0, 3 * LANES), pl.ds(0, LANES)]),
        (branch_hbm, branch.at[:, pl.ds(LANES, 3 * LANES), pl.ds(LANES, LANES)]),
        (merge_hbm, merge),
        (squeeze_hbm, squeeze),
        (excite_hbm, excite),
        (attend_hbm, attend),
        (score_hbm, score),
        (embed_hbm, embed),
        (lang_hbm, lang),
    ]
    loads = [
        pltpu.make_async_copy(source, target, load_sem.at[i])
        for i, (source, target) in enumerate(pairs)
    ]
    for load in loads:
        load.start()

    barrier = pltpu.get_barrier_semaphore()
    for step in range(1, groups):
        pl.semaphore_signal(
            barrier, inc=1, device_id=(lax.rem(me + step, groups), my_mem), device_id_type=MESH
        )
    for step in range(1, members):
        pl.semaphore_signal(
            barrier, inc=1, device_id=(me, lax.rem(my_mem + step, members)), device_id_type=MESH
        )

    staged[...] = jnp.zeros_like(staged)
    slots[...] = jnp.zeros_like(slots)
    w0[w0_hbm.shape[0] :, :] = jnp.zeros((WINDOW - w0_hbm.shape[0], channels), BF16)
    halo = 2 * groups
    half = rows_all // 2
    for buffer in (ping, pong):
        buffer[0, half:, :] = jnp.zeros((halo, LANES), BF16)
        buffer[1, :halo, :] = jnp.zeros((halo, LANES), BF16)
    empty = jnp.zeros((SCALE - 1, LANES, LANES), BF16)
    branch[:, 3 * LANES :, :LANES] = empty
    branch[:, :LANES, LANES:] = empty
    back[...] = jnp.zeros_like(back)

    loads[0].wait()
    for row in range(FLAT_ROWS):
        staged[pl.ds(row, stored, stride=SEND_ROWS), :] = bank[:, row * LANES : (row + 1) * LANES]

    def segment_for(group):
        picked = jnp.zeros((SEND_ROWS, LANES), F32)
        for s in range(stored):
            rows = staged[s * SEND_ROWS : (s + 1) * SEND_ROWS, :]
            picked = jnp.where(dest_ref[0, s] == group, rows, picked)
        return picked.astype(BF16)

    for step in range(1, groups):
        outbox[step] = segment_for(lax.rem(me + step, groups))

    pl.semaphore_wait(barrier, groups - 1 + members - 1)

    sends = []
    for step in range(1, groups):
        group = lax.rem(me + step, groups)
        copy = pltpu.make_async_remote_copy(
            src_ref=outbox.at[step],
            dst_ref=arrived.at[me],
            send_sem=out_send.at[step],
            recv_sem=out_recv.at[me],
            device_id=(group, my_mem),
            device_id_type=MESH,
        )
        copy.start()
        sends.append(copy)
    arrived[me] = segment_for(me)

    def place(slot):
        start = pl.multiple_of(slot * SLOT_ROWS + LEAD, 8)
        slots[pl.ds(start, SEND_ROWS), :] = arrived[slot].astype(F32)

    place(me)
    for step in range(1, groups):
        source = lax.rem(me + groups - step, groups)
        pltpu.make_async_remote_copy(
            src_ref=outbox.at[step],
            dst_ref=arrived.at[source],
            send_sem=out_send.at[step],
            recv_sem=out_recv.at[source],
            device_id=(source, my_mem),
            device_id_type=MESH,
        ).wait_recv()
        place(source)

    lane = lax.broadcasted_iota(jnp.int32, (groups, LANES), 1)

    def windows(block, _):
        first = block * 5
        held = {}

        def row_at(index):
            if index not in held:
                held[index] = slots[pl.ds(first + index, groups, stride=SLOT_ROWS), :]
            return held[index]

        pair = []
        for phase in range(8):
            begin = phase * MELS + LEAD * LANES - 2 * MELS
            index, offset = begin // LANES, begin % LANES
            pieces = []
            for j in range(4):
                low = row_at(index + j)
                if offset:
                    high = row_at(index + j + 1) if j < 3 else None
                    low = pltpu.roll(low, LANES - offset, 1)
                    if high is not None:
                        high = pltpu.roll(high, LANES - offset, 1)
                        low = jnp.where(lane < LANES - offset, low, high)
                if j == 3:
                    low = jnp.where(lane < TAPS0 * MELS - 3 * LANES, low, 0.0)
                pieces.append(low)
            pair.append(jnp.concatenate(pieces, axis=1))
            if len(pair) == 2:
                side, place_in = phase // 2 % 2, phase // 4
                start = pl.multiple_of(side * half + (block * 2 + place_in) * halo, 16)
                cols[pl.ds(start, 2 * groups), :] = jnp.concatenate(pair, axis=0).astype(BF16)
                pair = []
        return 0

    lax.fori_loop(0, FRAMES // 8, windows, 0)

    loads[1].wait()
    loads[2].wait()

    chunks = [slice(c, c + CHUNK) for c in range(0, channels, CHUNK)]
    narrow = [slice(c, c + LANES) for c in range(0, channels, LANES)]
    half_talls = talls // 2

    def first_layers(tile, _):
        rows = pl.ds(pl.multiple_of(tile * TALL, 16), TALL)
        for chunk in chunks:
            out = jnp.maximum(dot(cols[rows, :], w0[:, chunk]), 0.0)
            front[rows, chunk] = out.astype(BF16)
        side = tile // half_talls
        start = pl.multiple_of(tile % half_talls * TALL + side * halo, 16)
        for chunk in chunks:
            expanded = jnp.maximum(dot(front[rows, :], expand[:, chunk]), 0.0).astype(BF16)
            work[rows, chunk] = expanded
            if chunk.start == 0:
                ping[side, pl.ds(start, TALL), :] = expanded[:, LANES : 2 * LANES]
        return 0

    lax.fori_loop(0, talls, first_layers, 0)

    loads[3].wait()
    loads[4].wait()
    buffers = (ping, pong)
    for i in range(1, SCALE):
        source, target = buffers[(i - 1) % 2], buffers[i % 2]

        def one_branch(tile, _, i=i, source=source, target=target):
            start = pl.multiple_of(tile * TALL, 16)
            near, far = pl.ds(start, TALL), pl.ds(start + halo, TALL)
            window = jnp.concatenate(
                [source[1, near, :], source[0, near, :], source[1, far, :], source[0, far, :]], axis=1
            )
            out = jnp.maximum(dot(window, branch[i - 1]), 0.0).astype(BF16)
            for side, spot in ((0, near), (1, far)):
                rows = pl.ds(start + side * half, TALL)
                mine = out[:, side * LANES : (side + 1) * LANES]
                work[rows, i * LANES : (i + 1) * LANES] = mine
                if i < SCALE - 1:
                    following = work[rows, (i + 1) * LANES : (i + 2) * LANES].astype(F32)
                    target[side, spot, :] = (following + mine.astype(F32)).astype(BF16)
            return 0

        lax.fori_loop(0, half_talls, one_branch, 0, unroll=True)

    loads[5].wait()

    def by_frame(values):
        return values.reshape(values.shape[0] // groups, groups, values.shape[1])

    def merging(tile, total):
        rows = pl.ds(pl.multiple_of(tile * TALL, 16), TALL)
        sums = []
        for chunk in chunks:
            merged = jnp.maximum(dot(work[rows, :], merge[:, chunk]), 0.0)
            wide[rows, chunk] = merged
            sums.append(jnp.sum(by_frame(merged), axis=0))
        return total + jnp.concatenate(sums, axis=1)

    zeros = jnp.zeros((groups, channels), F32)
    total = lax.fori_loop(0, talls, merging, zeros)

    loads[6].wait()
    loads[7].wait()
    hidden = jnp.maximum(dot_split(total / FRAMES, squeeze[...]), 0.0)
    excited = 1.0 / (1.0 + jnp.exp(-dot_split(hidden, excite[...])))

    loads[8].wait()
    pivot = front[0 : 2 * groups, :].astype(F32)[:groups] + wide[0:groups, :] * excited

    def trunk_out(tile, carry):
        first, second = carry
        rows = pl.ds(pl.multiple_of(tile * TILE, 16), TILE)
        sums, squares = [], []
        for chunk in narrow:
            out = by_frame(wide[rows, chunk]) * excited[:, chunk]
            out = by_frame(front[rows, chunk].astype(F32)) + out
            work[rows, chunk] = out.reshape(TILE, LANES).astype(BF16)
            moved = out - pivot[:, chunk]
            sums.append(jnp.sum(moved, axis=0))
            squares.append(jnp.sum(moved * moved, axis=0))
        attn[rows, :] = dot(work[rows, :], attend[0:channels, :])
        return first + jnp.concatenate(sums, axis=1), second + jnp.concatenate(squares, axis=1)

    first, second = lax.fori_loop(0, tiles, trunk_out, (zeros, zeros))
    shift = first / FRAMES
    center = pivot + shift
    spread = jnp.sqrt(jnp.maximum(second / FRAMES - shift * shift, 0.0) + EPS_STAT)
    context = dot_split(center, attend[channels : 2 * channels, :]) + dot_split(
        spread, attend[2 * channels :, :]
    )

    loads[9].wait()

    inverse = 1.0 / spread

    def energies(tile, carry):
        rows = pl.ds(pl.multiple_of(tile * TILE, 16), TILE)
        attended = jnp.tanh(by_frame(attn[rows, :]) + context).reshape(TILE, -1).astype(BF16)
        parts = ([], [], [])
        for chunk in chunks:
            weights = by_frame(jnp.exp(dot(attended, score[:, chunk])))
            value = by_frame(work[rows, chunk].astype(F32))
            value = (value - center[:, chunk]) * inverse[:, chunk]
            parts[0].append(jnp.sum(weights, axis=0))
            weights = weights * value
            parts[1].append(jnp.sum(weights, axis=0))
            parts[2].append(jnp.sum(weights * value, axis=0))
        return tuple(c + jnp.concatenate(p, axis=1) for c, p in zip(carry, parts))

    norm, weighted, squared = lax.fori_loop(0, tiles, energies, (zeros, zeros, zeros))
    weighted = weighted / norm
    squared = jnp.maximum(squared / norm - weighted * weighted, 0.0)
    mean = center + spread * weighted
    deviation = jnp.sqrt(spread * spread * squared + EPS_STAT)

    loads[10].wait()
    loads[11].wait()
    pooled = jnp.concatenate([mean, deviation], axis=1).astype(BF16)
    embedding = lax.dot_general(
        pooled, embed[...], (((1,), (1,)), ((), ())), preferred_element_type=F32
    )
    scores = dot(embedding.astype(BF16), lang[...])
    width = embedding.shape[1]
    langs = scores.shape[1]
    back[:, 0, :] = embedding[:, :LANES]
    back[:, 1, : width - LANES] = embedding[:, LANES:]
    back[:, 2, :langs] = scores

    for step in range(1, groups):
        group = lax.rem(me + step, groups)
        copy = pltpu.make_async_remote_copy(
            src_ref=back.at[group],
            dst_ref=home.at[me],
            send_sem=back_send.at[step],
            recv_sem=back_recv.at[me],
            device_id=(group, my_mem),
            device_id_type=MESH,
        )
        copy.start()
        sends.append(copy)
    home[me] = back[me]
    for step in range(1, groups):
        source = lax.rem(me + groups - step, groups)
        pltpu.make_async_remote_copy(
            src_ref=back.at[source],
            dst_ref=home.at[source],
            send_sem=back_send.at[step],
            recv_sem=back_recv.at[source],
            device_id=(source, my_mem),
            device_id_type=MESH,
        ).wait_recv()
    for s in range(stored):
        picked = home[0]
        for group in range(1, groups):
            picked = jnp.where(dest_ref[0, s] == group, home[group], picked)
        own[s] = picked

    left, right = own[:, 0, :], own[:, 1, :]
    result_ref[:, :LANES] = own[:, 2, :]
    squares = jnp.sum(left * left + right * right, axis=1, keepdims=True)
    factor = lax.rsqrt(squares / width + EPS_NORM)
    mine = jnp.concatenate([left * factor, right * factor], axis=1).astype(BF16)
    normed[...] = mine.astype(F32)
    for step in range(1, members):
        member = lax.rem(my_mem + step, members)
        copy = pltpu.make_async_remote_copy(
            src_ref=normed,
            dst_ref=gathered.at[my_mem],
            send_sem=mem_send.at[step],
            recv_sem=mem_recv.at[my_mem],
            device_id=(me, member),
            device_id_type=MESH,
        )
        copy.start()
        sends.append(copy)
    gathered[my_mem] = normed[...]
    for step in range(1, members):
        source = lax.rem(my_mem + members - step, members)
        pltpu.make_async_remote_copy(
            src_ref=normed,
            dst_ref=gathered.at[source],
            send_sem=mem_send.at[step],
            recv_sem=mem_recv.at[source],
            device_id=(me, source),
            device_id_type=MESH,
        ).wait_recv()
    every = gathered[...].reshape(members * stored, 2 * LANES).astype(BF16)
    inner = lax.dot_general(mine, every, (((1,), (1,)), ((), ())), preferred_element_type=F32)
    result_ref[:, LANES : LANES + members * stored] = inner / width
    for copy in sends:
        copy.wait_send()


def split_result(result_ref, logits_ref, sim_ref):
    logits_ref[0] = result_ref[:, : logits_ref.shape[2]]
    sim_ref[0] = result_ref[:, LANES : LANES + sim_ref.shape[2]]


def shards(
    filterbank,
    destination,
    initial_conv_weight,
    expand_weight,
    branch_weight,
    merge_weight,
    squeeze_weight,
    excite_weight,
    attend_weight,
    score_weight,
    embed_weight,
    language_weight,
):
    groups = lax.axis_size("grp")
    members = lax.axis_size("mem")
    stored = filterbank.shape[2]
    rows = FRAMES * groups
    channels = expand_weight.shape[0]
    langs = language_weight.shape[2]
    operands = (
        filterbank.reshape(stored, FRAMES * MELS),
        destination,
        initial_conv_weight,
        expand_weight,
        branch_weight,
        merge_weight,
        squeeze_weight,
        excite_weight,
        attend_weight[0],
        score_weight[0],
        embed_weight[0].T,
        language_weight[0],
    )
    copied = [pltpu.VMEM(a.shape, a.dtype) for a in operands]
    del copied[1]
    copied[1] = pltpu.VMEM((WINDOW, channels), BF16)
    copied[3] = pltpu.VMEM((SCALE - 1, 4 * LANES, 2 * LANES), BF16)
    anywhere = pl.BlockSpec(memory_space=pl.ANY)
    in_specs = [anywhere] * len(operands)
    in_specs[1] = pl.BlockSpec(memory_space=pltpu.SMEM)
    dma = pltpu.SemaphoreType.DMA
    result = pl.pallas_call(
        functools.partial(kernel, groups, members),
        out_shape=jax.ShapeDtypeStruct((stored, 2 * LANES), F32),
        in_specs=in_specs,
        out_specs=pl.BlockSpec(memory_space=pltpu.VMEM),
        scratch_shapes=copied
        + [
            pltpu.VMEM((stored * SEND_ROWS, LANES), F32),
            pltpu.VMEM((groups, SEND_ROWS, LANES), BF16),
            pltpu.VMEM((groups, SEND_ROWS, LANES), BF16),
            pltpu.VMEM((groups * SLOT_ROWS, LANES), F32),
            pltpu.VMEM((rows, WINDOW), BF16),
            pltpu.VMEM((rows, channels), BF16),
            pltpu.VMEM((rows, channels), BF16),
            pltpu.VMEM((rows, channels), F32),
            pltpu.VMEM((2, rows // 2 + 2 * groups, LANES), BF16),
            pltpu.VMEM((2, rows // 2 + 2 * groups, LANES), BF16),
            pltpu.VMEM((rows, LANES), F32),
            pltpu.VMEM((groups, 8, LANES), F32),
            pltpu.VMEM((groups, 8, LANES), F32),
            pltpu.VMEM((stored, 8, LANES), F32),
            pltpu.VMEM((stored, 2 * LANES), F32),
            pltpu.VMEM((members, stored, 2 * LANES), F32),
            dma((len(copied) + 1,)),
            dma((groups,)),
            dma((groups,)),
            dma((groups,)),
            dma((groups,)),
            dma((members,)),
            dma((members,)),
        ],
        compiler_params=pltpu.CompilerParams(
            collective_id=0, has_side_effects=True, vmem_limit_bytes=60 * 1024 * 1024
        ),
        cost_estimate=pl.CostEstimate(
            flops=rows * 12_000_000, bytes_accessed=10_000_000, transcendentals=rows * 1200
        ),
    )(*operands)
    return pl.pallas_call(
        split_result,
        out_shape=(
            jax.ShapeDtypeStruct((1, stored, langs), F32),
            jax.ShapeDtypeStruct((1, stored, members * stored), F32),
        ),
    )(result)


def solution(mesh):
    return jax.shard_map(
        shards,
        mesh=mesh,
        in_specs=(
            P("grp", "mem", None, None),
            P("grp", "mem"),
            P(),
            P(),
            P(),
            P(),
            P(),
            P(),
            P("grp", None, None),
            P("grp", None, None),
            P("grp", None, None),
            P("grp", None, None),
        ),
        out_specs=(P("grp", "mem", None), P("grp", "mem", None)),
        check_vma=False,
    )
```

```python
import functools

import jax
import jax.numpy as jnp
from jax import lax
from jax.experimental import pallas as pl
from jax.experimental.pallas import tpu as pltpu
from jax.sharding import PartitionSpec as P

MELS = 80
SCALE = 8
FRAMES = 200
LANES = 128
FLAT_ROWS = 125
TAG_ROW = 127
PART_ROWS = 64
SEND_ROWS = 128
LEAD = 8
SLOT_ROWS = LEAD + SEND_ROWS
TAPS0 = 5
WINDOW = 512
TILE = 400
CHUNK = 256
EPS_STAT = 1e-05
EPS_NORM = 1e-06

MESH = pl.DeviceIdType.MESH
F32 = jnp.float32
BF16 = jnp.bfloat16


def dot(a, b):
    return jnp.dot(a, b, preferred_element_type=F32)


def dot_split(values, weight):
    rows = values.shape[0]
    high = values.astype(BF16).astype(F32)
    both = jnp.concatenate([high, values - high], axis=0).astype(BF16)
    product = dot(both, weight)
    return product[:rows] + product[rows:]


def kernel(
    groups,
    members,
    bank_hbm,
    dest_ref,
    w0_hbm,
    expand_hbm,
    branch_hbm,
    merge_hbm,
    squeeze_hbm,
    excite_hbm,
    attend_hbm,
    score_hbm,
    embed_hbm,
    lang_hbm,
    result_ref,
    bank,
    w0,
    expand,
    branch,
    merge,
    squeeze,
    excite,
    attend,
    score,
    embed,
    lang,
    staged,
    outbox,
    arrived,
    slots,
    cols,
    front,
    work,
    wide,
    ping,
    pong,
    attn,
    back,
    home,
    own,
    load_sem,
    out_send,
    out_recv,
    back_send,
    back_recv,
):
    stored = bank.shape[0]
    rows_all = FRAMES * groups
    tiles = rows_all // TILE
    channels = front.shape[1]
    me = lax.axis_index("grp")
    my_mem = lax.axis_index("mem")

    pairs = [
        (bank_hbm, bank),
        (w0_hbm, w0.at[pl.ds(0, w0_hbm.shape[0])]),
        (expand_hbm, expand),
        (branch_hbm, branch.at[:, pl.ds(0, 3 * LANES), pl.ds(0, LANES)]),
        (branch_hbm, branch.at[:, pl.ds(LANES, 3 * LANES), pl.ds(LANES, LANES)]),
        (merge_hbm, merge),
        (squeeze_hbm, squeeze),
        (excite_hbm, excite),
        (attend_hbm, attend),
        (score_hbm, score),
        (embed_hbm, embed),
        (lang_hbm, lang),
    ]
    loads = [
        pltpu.make_async_copy(source, target, load_sem.at[i])
        for i, (source, target) in enumerate(pairs)
    ]
    for load in loads:
        load.start()

    barrier = pltpu.get_barrier_semaphore()
    others = [(g, m) for m in range(members) for g in range(groups) if g or m]

    def other(group_step, member_step):
        return (lax.rem(me + group_step, groups), lax.rem(my_mem + member_step, members))

    for steps in others:
        pl.semaphore_signal(barrier, inc=1, device_id=other(*steps), device_id_type=MESH)

    staged[...] = jnp.zeros_like(staged)
    slots[...] = jnp.zeros_like(slots)
    w0[w0_hbm.shape[0] :, :] = jnp.zeros((WINDOW - w0_hbm.shape[0], channels), BF16)
    halo = 2 * groups
    half = rows_all // 2
    for buffer in (ping, pong):
        buffer[0, half:, :] = jnp.zeros((halo, LANES), BF16)
        buffer[1, :halo, :] = jnp.zeros((halo, LANES), BF16)
    empty = jnp.zeros((SCALE - 1, LANES, LANES), BF16)
    branch[:, 3 * LANES :, :LANES] = empty
    branch[:, :LANES, LANES:] = empty
    back[...] = jnp.zeros_like(back)

    for s in range(stored):
        staged[s * SEND_ROWS + TAG_ROW : s * SEND_ROWS + TAG_ROW + 1, :] = jnp.full(
            (1, LANES), s + 1, F32
        )

    def stage(first, last):
        for row in range(first, last):
            staged[pl.ds(row, stored, stride=SEND_ROWS), :] = bank[
                :, row * LANES : (row + 1) * LANES
            ]

    def part_for(group, part):
        picked = jnp.zeros((PART_ROWS, LANES), F32)
        for s in range(stored):
            first = s * SEND_ROWS + part * PART_ROWS
            rows = staged[first : first + PART_ROWS, :]
            picked = jnp.where(dest_ref[0, s] == group, rows, picked)
        return picked.astype(BF16)

    def fill(part):
        for step in range(1, groups):
            outbox[part, step] = part_for(lax.rem(me + step, groups), part)
        arrived[part, me] = part_for(me, part)

    def routed(part, step, source, group):
        return pltpu.make_async_remote_copy(
            src_ref=outbox.at[part, step],
            dst_ref=arrived.at[part, source],
            send_sem=out_send.at[part, step],
            recv_sem=out_recv.at[part, source],
            device_id=(group, my_mem),
            device_id_type=MESH,
        )

    sends = []

    def send(part):
        for step in range(1, groups):
            copy = routed(part, step, me, lax.rem(me + step, groups))
            copy.start()
            sends.append(copy)

    def place(part, slot):
        start = pl.multiple_of(slot * SLOT_ROWS + LEAD + part * PART_ROWS, 8)
        slots[pl.ds(start, PART_ROWS), :] = arrived[part, slot].astype(F32)

    def receive(part):
        place(part, me)
        for step in range(1, groups):
            source = lax.rem(me + groups - step, groups)
            routed(part, step, source, source).wait_recv()
            place(part, source)

    loads[0].wait()
    stage(0, PART_ROWS)
    fill(0)
    pl.semaphore_wait(barrier, len(others))
    send(0)
    stage(PART_ROWS, FLAT_ROWS)
    fill(1)
    send(1)

    lane = lax.broadcasted_iota(jnp.int32, (groups, LANES), 1)

    def windows(block, _, phases=range(8)):
        first = block * 5
        held = {}

        def row_at(index):
            if index not in held:
                held[index] = slots[pl.ds(first + index, groups, stride=SLOT_ROWS), :]
            return held[index]

        pair = []
        for phase in phases:
            begin = phase * MELS + LEAD * LANES - 2 * MELS
            index, offset = begin // LANES, begin % LANES
            pieces = []
            for j in range(4):
                low = row_at(index + j)
                if offset:
                    high = row_at(index + j + 1) if j < 3 else None
                    low = pltpu.roll(low, LANES - offset, 1)
                    if high is not None:
                        high = pltpu.roll(high, LANES - offset, 1)
                        low = jnp.where(lane < LANES - offset, low, high)
                if j == 3:
                    low = jnp.where(lane < TAPS0 * MELS - 3 * LANES, low, 0.0)
                pieces.append(low)
            pair.append(jnp.concatenate(pieces, axis=1))
            if len(pair) == 2:
                side, place_in = phase // 2 % 2, phase // 4
                start = pl.multiple_of(side * half + (block * 2 + place_in) * halo, 16)
                cols[pl.ds(start, 2 * groups), :] = jnp.concatenate(pair, axis=0).astype(BF16)
                pair = []
        return 0


    chunks = [slice(c, c + CHUNK) for c in range(0, channels, CHUNK)]
    narrow = [slice(c, c + LANES) for c in range(0, channels, LANES)]
    half_tiles = tiles // 2
    part_tiles = half_tiles // 2

    def first_layers(step, _, part):
        side = step // part_tiles
        start = side * half_tiles + part * part_tiles + step % part_tiles
        rows_of_tile(side, start)
        return 0

    def rows_of_tile(side, tile):
        rows = pl.ds(pl.multiple_of(tile * TILE, 16), TILE)
        for chunk in chunks:
            out = jnp.maximum(dot(cols[rows, :], w0[:, chunk]), 0.0)
            front[rows, chunk] = out.astype(BF16)
        start = pl.multiple_of(tile % half_tiles * TILE + side * halo, 16)
        for chunk in chunks:
            expanded = jnp.maximum(dot(front[rows, :], expand[:, chunk]), 0.0).astype(BF16)
            work[rows, chunk] = expanded
            if chunk.start == 0:
                ping[side, pl.ds(start, TILE), :] = expanded[:, LANES : 2 * LANES]

    split = FRAMES // 16
    receive(0)
    lax.fori_loop(0, split, windows, 0)
    windows(split, 0, range(4))
    loads[1].wait()
    loads[2].wait()
    lax.fori_loop(0, half_tiles, functools.partial(first_layers, part=0), 0)
    receive(1)
    windows(split, 0, range(4, 8))
    lax.fori_loop(split + 1, FRAMES // 8, windows, 0)
    lax.fori_loop(0, half_tiles, functools.partial(first_layers, part=1), 0)

    loads[3].wait()
    loads[4].wait()
    buffers = (ping, pong)
    for i in range(1, SCALE):
        source, target = buffers[(i - 1) % 2], buffers[i % 2]

        def one_branch(tile, _, i=i, source=source, target=target):
            start = pl.multiple_of(tile * TILE, 16)
            near, far = pl.ds(start, TILE), pl.ds(start + halo, TILE)
            window = jnp.concatenate(
                [source[1, near, :], source[0, near, :], source[1, far, :], source[0, far, :]], axis=1
            )
            out = jnp.maximum(dot(window, branch[i - 1]), 0.0).astype(BF16)
            for side, spot in ((0, near), (1, far)):
                rows = pl.ds(start + side * half, TILE)
                mine = out[:, side * LANES : (side + 1) * LANES]
                work[rows, i * LANES : (i + 1) * LANES] = mine
                if i < SCALE - 1:
                    following = work[rows, (i + 1) * LANES : (i + 2) * LANES].astype(F32)
                    target[side, spot, :] = (following + mine.astype(F32)).astype(BF16)
            return 0

        lax.fori_loop(0, half_tiles, one_branch, 0, unroll=True)

    loads[5].wait()

    def by_frame(values):
        return values.reshape(values.shape[0] // groups, groups, values.shape[1])

    def merging(tile, total):
        rows = pl.ds(pl.multiple_of(tile * TILE, 16), TILE)
        sums = []
        for chunk in chunks:
            merged = jnp.maximum(dot(work[rows, :], merge[:, chunk]), 0.0)
            wide[rows, chunk] = merged
            sums.append(jnp.sum(by_frame(merged), axis=0))
        return total + jnp.concatenate(sums, axis=1)

    zeros = jnp.zeros((groups, channels), F32)
    total = lax.fori_loop(0, tiles, merging, zeros)

    loads[6].wait()
    loads[7].wait()
    hidden = jnp.maximum(dot_split(total / FRAMES, squeeze[...]), 0.0)
    excited = 1.0 / (1.0 + jnp.exp(-dot_split(hidden, excite[...])))

    loads[8].wait()
    pivot = front[0 : 2 * groups, :].astype(F32)[:groups] + wide[0:groups, :] * excited

    def trunk_out(tile, carry):
        first, second = carry
        rows = pl.ds(pl.multiple_of(tile * TILE, 16), TILE)
        sums, squares = [], []
        for chunk in narrow:
            out = by_frame(wide[rows, chunk]) * excited[:, chunk]
            out = by_frame(front[rows, chunk].astype(F32)) + out
            work[rows, chunk] = out.reshape(TILE, LANES).astype(BF16)
            moved = out - pivot[:, chunk]
            sums.append(jnp.sum(moved, axis=0))
            squares.append(jnp.sum(moved * moved, axis=0))
        attn[rows, :] = dot(work[rows, :], attend[0:channels, :])
        return first + jnp.concatenate(sums, axis=1), second + jnp.concatenate(squares, axis=1)

    first, second = lax.fori_loop(0, tiles, trunk_out, (zeros, zeros))
    shift = first / FRAMES
    center = pivot + shift
    spread = jnp.sqrt(jnp.maximum(second / FRAMES - shift * shift, 0.0) + EPS_STAT)
    context = dot_split(center, attend[channels : 2 * channels, :]) + dot_split(
        spread, attend[2 * channels :, :]
    )

    loads[9].wait()

    inverse = 1.0 / spread

    def energies(tile, carry):
        rows = pl.ds(pl.multiple_of(tile * TILE, 16), TILE)
        attended = jnp.tanh(by_frame(attn[rows, :]) + context).reshape(TILE, -1).astype(BF16)
        parts = ([], [], [])
        for chunk in chunks:
            weights = by_frame(jnp.exp(dot(attended, score[:, chunk])))
            value = by_frame(work[rows, chunk].astype(F32))
            value = (value - center[:, chunk]) * inverse[:, chunk]
            parts[0].append(jnp.sum(weights, axis=0))
            weights = weights * value
            parts[1].append(jnp.sum(weights, axis=0))
            parts[2].append(jnp.sum(weights * value, axis=0))
        return tuple(c + jnp.concatenate(p, axis=1) for c, p in zip(carry, parts))

    norm, weighted, squared = lax.fori_loop(0, tiles, energies, (zeros, zeros, zeros))
    weighted = weighted / norm
    squared = jnp.maximum(squared / norm - weighted * weighted, 0.0)
    mean = center + spread * weighted
    deviation = jnp.sqrt(spread * spread * squared + EPS_STAT)

    loads[10].wait()
    loads[11].wait()
    pooled = jnp.concatenate([mean, deviation], axis=1).astype(BF16)
    embedding = lax.dot_general(
        pooled, embed[...], (((1,), (1,)), ((), ())), preferred_element_type=F32
    )
    scores = dot(embedding.astype(BF16), lang[...])
    width = embedding.shape[1]
    langs = scores.shape[1]
    squares = jnp.sum(embedding * embedding, axis=1, keepdims=True)
    factor = lax.rsqrt(squares / width + EPS_NORM)
    normed = (embedding * factor).astype(BF16).astype(F32)
    back[:, 0, :] = normed[:, :LANES]
    back[:, 1, : width - LANES] = normed[:, LANES:]
    back[:, 2, :langs] = scores
    back[:, 3, :] = slots[pl.ds(LEAD + TAG_ROW, groups, stride=SLOT_ROWS), :]

    def returned(group_step, member_step, source, target):
        return pltpu.make_async_remote_copy(
            src_ref=back.at[target[0]],
            dst_ref=home.at[source[1], source[0]],
            send_sem=back_send.at[member_step, group_step],
            recv_sem=back_recv.at[source[1], source[0]],
            device_id=target,
            device_id_type=MESH,
        )

    for steps in others:
        copy = returned(*steps, (me, my_mem), other(*steps))
        copy.start()
        sends.append(copy)
    home[my_mem, me] = back[me]
    for group_step, member_step in others:
        source = (
            lax.rem(me + groups - group_step, groups),
            lax.rem(my_mem + members - member_step, members),
        )
        returned(group_step, member_step, source, source).wait_recv()

    for s in range(stored):
        picked = home[my_mem, 0]
        for group in range(1, groups):
            picked = jnp.where(dest_ref[0, s] == group, home[my_mem, group], picked)
        own[s] = picked
    result_ref[:, :LANES] = own[:, 2, :]
    mine = jnp.concatenate([own[:, 0, :], own[:, 1, :]], axis=1).astype(BF16)
    count = members * groups
    every = home[...].reshape(count, 8, LANES)
    placed = jnp.concatenate([every[:, 0, :], every[:, 1, :]], axis=1).astype(BF16)
    inner = lax.dot_general(mine, placed, (((1,), (1,)), ((), ())), preferred_element_type=F32)
    slot = lax.broadcasted_iota(jnp.int32, (count, LANES), 0)
    column = lax.broadcasted_iota(jnp.int32, (count, LANES), 1)
    tags = every[:, 3, :]
    wanted = (column - slot // groups * stored + 1).astype(F32)
    chosen = jnp.where((tags > 0.0) & (tags == wanted), 1.0, 0.0).astype(BF16)
    result_ref[:, LANES:] = dot_split(inner / width, chosen)
    for copy in sends:
        copy.wait_send()


def split_result(result_ref, logits_ref, sim_ref):
    logits_ref[0] = result_ref[:, : logits_ref.shape[2]]
    sim_ref[0] = result_ref[:, LANES : LANES + sim_ref.shape[2]]


def shards(
    filterbank,
    destination,
    initial_conv_weight,
    expand_weight,
    branch_weight,
    merge_weight,
    squeeze_weight,
    excite_weight,
    attend_weight,
    score_weight,
    embed_weight,
    language_weight,
):
    groups = lax.axis_size("grp")
    members = lax.axis_size("mem")
    stored = filterbank.shape[2]
    rows = FRAMES * groups
    channels = expand_weight.shape[0]
    langs = language_weight.shape[2]
    operands = (
        filterbank.reshape(stored, FRAMES * MELS),
        destination,
        initial_conv_weight,
        expand_weight,
        branch_weight,
        merge_weight,
        squeeze_weight,
        excite_weight,
        attend_weight[0],
        score_weight[0],
        embed_weight[0].T,
        language_weight[0],
    )
    copied = [pltpu.VMEM(a.shape, a.dtype) for a in operands]
    del copied[1]
    copied[1] = pltpu.VMEM((WINDOW, channels), BF16)
    copied[3] = pltpu.VMEM((SCALE - 1, 4 * LANES, 2 * LANES), BF16)
    anywhere = pl.BlockSpec(memory_space=pl.ANY)
    in_specs = [anywhere] * len(operands)
    in_specs[1] = pl.BlockSpec(memory_space=pltpu.SMEM)
    dma = pltpu.SemaphoreType.DMA
    result = pl.pallas_call(
        functools.partial(kernel, groups, members),
        out_shape=jax.ShapeDtypeStruct((stored, 2 * LANES), F32),
        in_specs=in_specs,
        out_specs=pl.BlockSpec(memory_space=pltpu.VMEM),
        scratch_shapes=copied
        + [
            pltpu.VMEM((stored * SEND_ROWS, LANES), F32),
            pltpu.VMEM((2, groups, PART_ROWS, LANES), BF16),
            pltpu.VMEM((2, groups, PART_ROWS, LANES), BF16),
            pltpu.VMEM((groups * SLOT_ROWS, LANES), F32),
            pltpu.VMEM((rows, WINDOW), BF16),
            pltpu.VMEM((rows, channels), BF16),
            pltpu.VMEM((rows, channels), BF16),
            pltpu.VMEM((rows, channels), F32),
            pltpu.VMEM((2, rows // 2 + 2 * groups, LANES), BF16),
            pltpu.VMEM((2, rows // 2 + 2 * groups, LANES), BF16),
            pltpu.VMEM((rows, LANES), F32),
            pltpu.VMEM((groups, 8, LANES), F32),
            pltpu.VMEM((members, groups, 8, LANES), F32),
            pltpu.VMEM((stored, 8, LANES), F32),
            dma((len(copied) + 1,)),
            dma((2, groups)),
            dma((2, groups)),
            dma((members, groups)),
            dma((members, groups)),
        ],
        compiler_params=pltpu.CompilerParams(
            collective_id=0, has_side_effects=True, vmem_limit_bytes=60 * 1024 * 1024
        ),
        cost_estimate=pl.CostEstimate(
            flops=rows * 12_000_000, bytes_accessed=10_000_000, transcendentals=rows * 1200
        ),
    )(*operands)
    return pl.pallas_call(
        split_result,
        out_shape=(
            jax.ShapeDtypeStruct((1, stored, langs), F32),
            jax.ShapeDtypeStruct((1, stored, members * stored), F32),
        ),
    )(result)


def solution(mesh):
    return jax.shard_map(
        shards,
        mesh=mesh,
        in_specs=(
            P("grp", "mem", None, None),
            P("grp", "mem"),
            P(),
            P(),
            P(),
            P(),
            P(),
            P(),
            P("grp", None, None),
            P("grp", None, None),
            P("grp", None, None),
            P("grp", None, None),
        ),
        out_specs=(P("grp", "mem", None), P("grp", "mem", None)),
        check_vma=False,
    )
```

```python
import functools

import jax
import jax.numpy as jnp
from jax import lax
from jax.experimental import pallas as pl
from jax.experimental.pallas import tpu as pltpu
from jax.sharding import PartitionSpec as P

MELS = 80
SCALE = 8
FRAMES = 200
LANES = 128
FLAT_ROWS = 125
TAG_ROW = 127
PART_ROWS = 64
SEND_ROWS = 128
LEAD = 8
SLOT_ROWS = LEAD + SEND_ROWS
TAPS0 = 5
WINDOW = 512
TILE = 400
CHUNK = 256
SHORT = 160
PIECE = 16
EPS_STAT = 1e-05
EPS_NORM = 1e-06

MESH = pl.DeviceIdType.MESH
F32 = jnp.float32
BF16 = jnp.bfloat16


def dot(a, b):
    return jnp.dot(a, b, preferred_element_type=F32)


def dot_split(values, weight):
    rows = values.shape[0]
    high = values.astype(BF16).astype(F32)
    both = jnp.concatenate([high, values - high], axis=0).astype(BF16)
    product = dot(both, weight)
    return product[:rows] + product[rows:]


def kernel(
    groups,
    members,
    bank_hbm,
    dest_ref,
    w0_hbm,
    expand_hbm,
    branch_hbm,
    merge_hbm,
    squeeze_hbm,
    excite_hbm,
    attend_hbm,
    score_hbm,
    embed_hbm,
    lang_hbm,
    result_ref,
    bank,
    w0,
    expand,
    branch,
    merge,
    squeeze,
    excite,
    attend,
    score,
    embed,
    lang,
    staged,
    outbox,
    arrived,
    slots,
    cols,
    front,
    work,
    wide,
    ping,
    pong,
    attn,
    back,
    home,
    own,
    load_sem,
    out_send,
    out_recv,
    back_send,
    back_recv,
):
    stored = bank.shape[0]
    rows_all = FRAMES * groups
    tiles = rows_all // TILE
    channels = front.shape[1]
    me = lax.axis_index("grp")
    my_mem = lax.axis_index("mem")

    pairs = [
        (bank_hbm, bank),
        (w0_hbm, w0.at[pl.ds(0, w0_hbm.shape[0])]),
        (expand_hbm, expand),
        (branch_hbm, branch.at[:, pl.ds(0, 3 * LANES), pl.ds(0, LANES)]),
        (branch_hbm, branch.at[:, pl.ds(LANES, 3 * LANES), pl.ds(LANES, LANES)]),
        (merge_hbm, merge),
        (squeeze_hbm, squeeze),
        (excite_hbm, excite),
        (attend_hbm, attend),
        (score_hbm, score),
        (embed_hbm, embed),
        (lang_hbm, lang),
    ]
    loads = [
        pltpu.make_async_copy(source, target, load_sem.at[i])
        for i, (source, target) in enumerate(pairs)
    ]
    for load in loads:
        load.start()

    barrier = pltpu.get_barrier_semaphore()
    others = [(g, m) for m in range(members) for g in range(groups) if g or m]

    def other(group_step, member_step):
        return (lax.rem(me + group_step, groups), lax.rem(my_mem + member_step, members))

    for steps in others:
        pl.semaphore_signal(barrier, inc=1, device_id=other(*steps), device_id_type=MESH)

    staged[...] = jnp.zeros_like(staged)
    slots[...] = jnp.zeros_like(slots)
    w0[w0_hbm.shape[0] :, :] = jnp.zeros((WINDOW - w0_hbm.shape[0], channels), BF16)
    halo = 2 * groups
    half = rows_all // 2
    for buffer in (ping, pong):
        buffer[0, half:, :] = jnp.zeros((halo, LANES), BF16)
        buffer[1, :halo, :] = jnp.zeros((halo, LANES), BF16)
    empty = jnp.zeros((SCALE - 1, LANES, LANES), BF16)
    branch[:, 3 * LANES :, :LANES] = empty
    branch[:, :LANES, LANES:] = empty
    back[...] = jnp.zeros_like(back)

    for s in range(stored):
        staged[s * SEND_ROWS + TAG_ROW : s * SEND_ROWS + TAG_ROW + 1, :] = jnp.full(
            (1, LANES), s + 1, F32
        )

    def stage(first, last):
        for row in range(first, last):
            staged[pl.ds(row, stored, stride=SEND_ROWS), :] = bank[
                :, row * LANES : (row + 1) * LANES
            ]

    def part_for(group, part):
        picked = jnp.zeros((PART_ROWS, LANES), F32)
        for s in range(stored):
            first = s * SEND_ROWS + part * PART_ROWS
            rows = staged[first : first + PART_ROWS, :]
            picked = jnp.where(dest_ref[0, s] == group, rows, picked)
        return picked.astype(BF16)

    def fill(part):
        for step in range(1, groups):
            outbox[part, step] = part_for(lax.rem(me + step, groups), part)
        arrived[part, me] = part_for(me, part)

    def routed(part, step, source, group):
        return pltpu.make_async_remote_copy(
            src_ref=outbox.at[part, step],
            dst_ref=arrived.at[part, source],
            send_sem=out_send.at[part, step],
            recv_sem=out_recv.at[part, source],
            device_id=(group, my_mem),
            device_id_type=MESH,
        )

    sends = []

    def send(part):
        for step in range(1, groups):
            copy = routed(part, step, me, lax.rem(me + step, groups))
            copy.start()
            sends.append(copy)

    def place(part, slot):
        start = pl.multiple_of(slot * SLOT_ROWS + LEAD + part * PART_ROWS, 8)
        slots[pl.ds(start, PART_ROWS), :] = arrived[part, slot].astype(F32)

    def receive(part):
        place(part, me)
        for step in range(1, groups):
            source = lax.rem(me + groups - step, groups)
            routed(part, step, source, source).wait_recv()
            place(part, source)

    loads[0].wait()
    stage(0, PART_ROWS)
    fill(0)
    pl.semaphore_wait(barrier, len(others))
    send(0)
    stage(PART_ROWS, FLAT_ROWS)
    fill(1)
    send(1)

    lane = lax.broadcasted_iota(jnp.int32, (groups, LANES), 1)

    def windows(block, _, phases=range(8)):
        first = block * 5
        held = {}

        def row_at(index):
            if index not in held:
                held[index] = slots[pl.ds(first + index, groups, stride=SLOT_ROWS), :]
            return held[index]

        pair = []
        for phase in phases:
            begin = phase * MELS + LEAD * LANES - 2 * MELS
            index, offset = begin // LANES, begin % LANES
            pieces = []
            for j in range(4):
                low = row_at(index + j)
                if offset:
                    high = row_at(index + j + 1) if j < 3 else None
                    low = pltpu.roll(low, LANES - offset, 1)
                    if high is not None:
                        high = pltpu.roll(high, LANES - offset, 1)
                        low = jnp.where(lane < LANES - offset, low, high)
                if j == 3:
                    low = jnp.where(lane < TAPS0 * MELS - 3 * LANES, low, 0.0)
                pieces.append(low)
            pair.append(jnp.concatenate(pieces, axis=1))
            if len(pair) == 2:
                side, place_in = phase // 2 % 2, phase // 4
                start = pl.multiple_of(side * half + (block * 2 + place_in) * halo, 16)
                cols[pl.ds(start, 2 * groups), :] = jnp.concatenate(pair, axis=0).astype(BF16)
                pair = []
        return 0


    chunks = [slice(c, c + CHUNK) for c in range(0, channels, CHUNK)]
    narrow = [slice(c, c + LANES) for c in range(0, channels, LANES)]
    half_tiles = tiles // 2
    part_tiles = half_tiles // 2

    def first_layers(step, _, part):
        side = step // part_tiles
        start = side * half_tiles + part * part_tiles + step % part_tiles
        rows_of_tile(side, start)
        return 0

    def rows_of_tile(side, tile):
        rows = pl.ds(pl.multiple_of(tile * TILE, 16), TILE)
        for chunk in chunks:
            out = jnp.maximum(dot(cols[rows, :], w0[:, chunk]), 0.0)
            front[rows, chunk] = out.astype(BF16)
        start = pl.multiple_of(tile % half_tiles * TILE + side * halo, 16)
        for chunk in chunks:
            expanded = jnp.maximum(dot(front[rows, :], expand[:, chunk]), 0.0).astype(BF16)
            work[rows, chunk] = expanded
            if chunk.start == 0:
                ping[side, pl.ds(start, TILE), :] = expanded[:, LANES : 2 * LANES]

    split = FRAMES // 16
    receive(0)
    lax.fori_loop(0, split, windows, 0)
    windows(split, 0, range(4))
    loads[1].wait()
    loads[2].wait()
    lax.fori_loop(0, half_tiles, functools.partial(first_layers, part=0), 0)
    receive(1)
    windows(split, 0, range(4, 8))
    lax.fori_loop(split + 1, FRAMES // 8, windows, 0)
    lax.fori_loop(0, half_tiles, functools.partial(first_layers, part=1), 0)

    loads[3].wait()
    loads[4].wait()
    buffers = (ping, pong)
    for i in range(1, SCALE):
        source, target = buffers[(i - 1) % 2], buffers[i % 2]

        def one_branch(tile, _, i=i, source=source, target=target):
            start = pl.multiple_of(tile * TILE, 16)
            near, far = pl.ds(start, TILE), pl.ds(start + halo, TILE)
            window = jnp.concatenate(
                [source[1, near, :], source[0, near, :], source[1, far, :], source[0, far, :]], axis=1
            )
            out = jnp.maximum(dot(window, branch[i - 1]), 0.0).astype(BF16)
            for side, spot in ((0, near), (1, far)):
                rows = pl.ds(start + side * half, TILE)
                mine = out[:, side * LANES : (side + 1) * LANES]
                work[rows, i * LANES : (i + 1) * LANES] = mine
                if i < SCALE - 1:
                    following = work[rows, (i + 1) * LANES : (i + 2) * LANES].astype(F32)
                    target[side, spot, :] = (following + mine.astype(F32)).astype(BF16)
            return 0

        lax.fori_loop(0, half_tiles, one_branch, 0, unroll=True)

    loads[5].wait()

    def by_frame(values):
        return values.reshape(values.shape[0] // groups, groups, values.shape[1])

    def merging(tile, total):
        start = pl.multiple_of(tile * TILE, 16)
        rows = pl.ds(start, TILE)
        sums = []
        for chunk in chunks:
            product = dot(work[rows, :], merge[:, chunk])
            for lanes in range(0, CHUNK, LANES):
                column = slice(chunk.start + lanes, chunk.start + lanes + LANES)
                part = jnp.zeros((groups, LANES), F32)
                for piece in range(0, TILE, PIECE):
                    merged = jnp.maximum(product[piece : piece + PIECE, lanes : lanes + LANES], 0.0)
                    wide[pl.ds(start + piece, PIECE), column] = merged
                    part = part + jnp.sum(by_frame(merged), axis=0)
                sums.append(part)
        return total + jnp.concatenate(sums, axis=1)

    zeros = jnp.zeros((groups, channels), F32)
    total = lax.fori_loop(0, tiles, merging, zeros)

    loads[6].wait()
    loads[7].wait()
    hidden = jnp.maximum(dot_split(total / FRAMES, squeeze[...]), 0.0)
    excited = 1.0 / (1.0 + jnp.exp(-dot_split(hidden, excite[...])))

    loads[8].wait()
    pivot = front[0 : 2 * groups, :].astype(F32)[:groups] + wide[0:groups, :] * excited

    def trunk_out(tile, carry):
        first, second = carry
        start = pl.multiple_of(tile * SHORT, 16)
        sums, squares = [], []
        for column in narrow:
            gain, middle = excited[:, column], pivot[:, column]
            part = jnp.zeros((groups, LANES), F32)
            square = part
            for piece in range(0, SHORT, PIECE):
                rows = pl.ds(start + piece, PIECE)
                out = by_frame(front[rows, column].astype(F32)) + by_frame(wide[rows, column]) * gain
                work[rows, column] = out.reshape(PIECE, LANES).astype(BF16)
                moved = out - middle
                part = part + jnp.sum(moved, axis=0)
                square = square + jnp.sum(moved * moved, axis=0)
            sums.append(part)
            squares.append(square)
        rows = pl.ds(start, SHORT)
        attn[rows, :] = dot(work[rows, :], attend[0:channels, :])
        return first + jnp.concatenate(sums, axis=1), second + jnp.concatenate(squares, axis=1)

    first, second = lax.fori_loop(0, rows_all // SHORT, trunk_out, (zeros, zeros))
    shift = first / FRAMES
    center = pivot + shift
    spread = jnp.sqrt(jnp.maximum(second / FRAMES - shift * shift, 0.0) + EPS_STAT)
    context = dot_split(center, attend[channels : 2 * channels, :]) + dot_split(
        spread, attend[2 * channels :, :]
    )

    loads[9].wait()

    inverse = 1.0 / spread

    def energies(tile, carry):
        start = pl.multiple_of(tile * SHORT, 16)
        rows = pl.ds(start, SHORT)
        attended = jnp.tanh(by_frame(attn[rows, :]) + context).reshape(SHORT, LANES).astype(BF16)
        parts = ([], [], [])
        for chunk in chunks:
            product = dot(attended, score[:, chunk])
            for lanes in range(0, CHUNK, LANES):
                column = slice(chunk.start + lanes, chunk.start + lanes + LANES)
                middle, gain = center[:, column], inverse[:, column]
                sums = [jnp.zeros((groups, LANES), F32)] * 3
                for piece in range(0, SHORT, PIECE):
                    weights = by_frame(
                        jnp.exp(product[piece : piece + PIECE, lanes : lanes + LANES])
                    )
                    value = by_frame(work[pl.ds(start + piece, PIECE), column].astype(F32))
                    value = (value - middle) * gain
                    once = weights * value
                    for k, term in enumerate((weights, once, once * value)):
                        sums[k] = sums[k] + jnp.sum(term, axis=0)
                for k in range(3):
                    parts[k].append(sums[k])
        return tuple(c + jnp.concatenate(p, axis=1) for c, p in zip(carry, parts))

    norm, weighted, squared = lax.fori_loop(0, rows_all // SHORT, energies, (zeros, zeros, zeros))
    weighted = weighted / norm
    squared = jnp.maximum(squared / norm - weighted * weighted, 0.0)
    mean = center + spread * weighted
    deviation = jnp.sqrt(spread * spread * squared + EPS_STAT)

    loads[10].wait()
    loads[11].wait()
    pooled = jnp.concatenate([mean, deviation], axis=1).astype(BF16)
    embedding = lax.dot_general(
        pooled, embed[...], (((1,), (1,)), ((), ())), preferred_element_type=F32
    )
    scores = dot(embedding.astype(BF16), lang[...])
    width = embedding.shape[1]
    langs = scores.shape[1]
    squares = jnp.sum(embedding * embedding, axis=1, keepdims=True)
    factor = lax.rsqrt(squares / width + EPS_NORM)
    normed = (embedding * factor).astype(BF16).astype(F32)
    back[:, 0, :] = normed[:, :LANES]
    back[:, 1, : width - LANES] = normed[:, LANES:]
    back[:, 2, :langs] = scores
    back[:, 3, :] = slots[pl.ds(LEAD + TAG_ROW, groups, stride=SLOT_ROWS), :]

    def returned(group_step, member_step, source, target):
        return pltpu.make_async_remote_copy(
            src_ref=back.at[target[0]],
            dst_ref=home.at[source[1], source[0]],
            send_sem=back_send.at[member_step, group_step],
            recv_sem=back_recv.at[source[1], source[0]],
            device_id=target,
            device_id_type=MESH,
        )

    for steps in others:
        copy = returned(*steps, (me, my_mem), other(*steps))
        copy.start()
        sends.append(copy)
    home[my_mem, me] = back[me]
    for group_step, member_step in others:
        source = (
            lax.rem(me + groups - group_step, groups),
            lax.rem(my_mem + members - member_step, members),
        )
        returned(group_step, member_step, source, source).wait_recv()

    for s in range(stored):
        picked = home[my_mem, 0]
        for group in range(1, groups):
            picked = jnp.where(dest_ref[0, s] == group, home[my_mem, group], picked)
        own[s] = picked
    result_ref[:, :LANES] = own[:, 2, :]
    mine = jnp.concatenate([own[:, 0, :], own[:, 1, :]], axis=1).astype(BF16)
    count = members * groups
    every = home[...].reshape(count, 8, LANES)
    placed = jnp.concatenate([every[:, 0, :], every[:, 1, :]], axis=1).astype(BF16)
    inner = lax.dot_general(mine, placed, (((1,), (1,)), ((), ())), preferred_element_type=F32)
    slot = lax.broadcasted_iota(jnp.int32, (count, LANES), 0)
    column = lax.broadcasted_iota(jnp.int32, (count, LANES), 1)
    tags = every[:, 3, :]
    wanted = (column - slot // groups * stored + 1).astype(F32)
    chosen = jnp.where((tags > 0.0) & (tags == wanted), 1.0, 0.0).astype(BF16)
    result_ref[:, LANES:] = dot_split(inner / width, chosen)
    for copy in sends:
        copy.wait_send()


def split_result(result_ref, logits_ref, sim_ref):
    logits_ref[0] = result_ref[:, : logits_ref.shape[2]]
    sim_ref[0] = result_ref[:, LANES : LANES + sim_ref.shape[2]]


def shards(
    filterbank,
    destination,
    initial_conv_weight,
    expand_weight,
    branch_weight,
    merge_weight,
    squeeze_weight,
    excite_weight,
    attend_weight,
    score_weight,
    embed_weight,
    language_weight,
):
    groups = lax.axis_size("grp")
    members = lax.axis_size("mem")
    stored = filterbank.shape[2]
    rows = FRAMES * groups
    channels = expand_weight.shape[0]
    langs = language_weight.shape[2]
    operands = (
        filterbank.reshape(stored, FRAMES * MELS),
        destination,
        initial_conv_weight,
        expand_weight,
        branch_weight,
        merge_weight,
        squeeze_weight,
        excite_weight,
        attend_weight[0],
        score_weight[0],
        embed_weight[0].T,
        language_weight[0],
    )
    copied = [pltpu.VMEM(a.shape, a.dtype) for a in operands]
    del copied[1]
    copied[1] = pltpu.VMEM((WINDOW, channels), BF16)
    copied[3] = pltpu.VMEM((SCALE - 1, 4 * LANES, 2 * LANES), BF16)
    anywhere = pl.BlockSpec(memory_space=pl.ANY)
    in_specs = [anywhere] * len(operands)
    in_specs[1] = pl.BlockSpec(memory_space=pltpu.SMEM)
    dma = pltpu.SemaphoreType.DMA
    result = pl.pallas_call(
        functools.partial(kernel, groups, members),
        out_shape=jax.ShapeDtypeStruct((stored, 2 * LANES), F32),
        in_specs=in_specs,
        out_specs=pl.BlockSpec(memory_space=pltpu.VMEM),
        scratch_shapes=copied
        + [
            pltpu.VMEM((stored * SEND_ROWS, LANES), F32),
            pltpu.VMEM((2, groups, PART_ROWS, LANES), BF16),
            pltpu.VMEM((2, groups, PART_ROWS, LANES), BF16),
            pltpu.VMEM((groups * SLOT_ROWS, LANES), F32),
            pltpu.VMEM((rows, WINDOW), BF16),
            pltpu.VMEM((rows, channels), BF16),
            pltpu.VMEM((rows, channels), BF16),
            pltpu.VMEM((rows, channels), F32),
            pltpu.VMEM((2, rows // 2 + 2 * groups, LANES), BF16),
            pltpu.VMEM((2, rows // 2 + 2 * groups, LANES), BF16),
            pltpu.VMEM((rows, LANES), F32),
            pltpu.VMEM((groups, 8, LANES), F32),
            pltpu.VMEM((members, groups, 8, LANES), F32),
            pltpu.VMEM((stored, 8, LANES), F32),
            dma((len(copied) + 1,)),
            dma((2, groups)),
            dma((2, groups)),
            dma((members, groups)),
            dma((members, groups)),
        ],
        compiler_params=pltpu.CompilerParams(
            collective_id=0, has_side_effects=True, vmem_limit_bytes=60 * 1024 * 1024
        ),
        cost_estimate=pl.CostEstimate(
            flops=rows * 12_000_000, bytes_accessed=10_000_000, transcendentals=rows * 1200
        ),
    )(*operands)
    return pl.pallas_call(
        split_result,
        out_shape=(
            jax.ShapeDtypeStruct((1, stored, langs), F32),
            jax.ShapeDtypeStruct((1, stored, members * stored), F32),
        ),
    )(result)


def solution(mesh):
    return jax.shard_map(
        shards,
        mesh=mesh,
        in_specs=(
            P("grp", "mem", None, None),
            P("grp", "mem"),
            P(),
            P(),
            P(),
            P(),
            P(),
            P(),
            P("grp", None, None),
            P("grp", None, None),
            P("grp", None, None),
            P("grp", None, None),
        ),
        out_specs=(P("grp", "mem", None), P("grp", "mem", None)),
        check_vma=False,
    )
```

```python
import functools

import jax
import jax.numpy as jnp
from jax import lax
from jax.experimental import pallas as pl
from jax.experimental.pallas import tpu as pltpu
from jax.sharding import PartitionSpec as P

MELS = 80
SCALE = 8
FRAMES = 200
LANES = 128
FLAT_ROWS = 125
PART_ROWS = 64
SEND_ROWS = 128
LEAD = 8
SLOT_ROWS = LEAD + SEND_ROWS
TAPS0 = 5
WINDOW = 512
TILE = 400
CHUNK = 256
EPS_STAT = 1e-05
EPS_NORM = 1e-06

MESH = pl.DeviceIdType.MESH
F32 = jnp.float32
BF16 = jnp.bfloat16


def dot(a, b):
    return jnp.dot(a, b, preferred_element_type=F32)


def dot_split(values, weight):
    rows = values.shape[0]
    high = values.astype(BF16).astype(F32)
    both = jnp.concatenate([high, values - high], axis=0).astype(BF16)
    product = dot(both, weight)
    return product[:rows] + product[rows:]


def kernel(
    groups,
    members,
    bank_hbm,
    dest_ref,
    w0_hbm,
    expand_hbm,
    branch_hbm,
    merge_hbm,
    squeeze_hbm,
    excite_hbm,
    attend_hbm,
    score_hbm,
    embed_hbm,
    lang_hbm,
    result_ref,
    bank,
    w0,
    expand,
    branch,
    merge,
    squeeze,
    excite,
    attend,
    score,
    embed,
    lang,
    staged,
    outbox,
    arrived,
    slots,
    cols,
    front,
    work,
    wide,
    ping,
    pong,
    attn,
    back,
    home,
    own,
    normed,
    gathered,
    load_sem,
    out_send,
    out_recv,
    back_send,
    back_recv,
    mem_send,
    mem_recv,
):
    stored = bank.shape[0]
    rows_all = FRAMES * groups
    tiles = rows_all // TILE
    channels = front.shape[1]
    me = lax.axis_index("grp")
    my_mem = lax.axis_index("mem")

    pairs = [
        (bank_hbm, bank),
        (w0_hbm, w0.at[pl.ds(0, w0_hbm.shape[0])]),
        (expand_hbm, expand),
        (branch_hbm, branch.at[:, pl.ds(0, 3 * LANES), pl.ds(0, LANES)]),
        (branch_hbm, branch.at[:, pl.ds(LANES, 3 * LANES), pl.ds(LANES, LANES)]),
        (merge_hbm, merge),
        (squeeze_hbm, squeeze),
        (excite_hbm, excite),
        (attend_hbm, attend),
        (score_hbm, score),
        (embed_hbm, embed),
        (lang_hbm, lang),
    ]
    loads = [
        pltpu.make_async_copy(source, target, load_sem.at[i])
        for i, (source, target) in enumerate(pairs)
    ]
    loads[0].start()

    barrier = pltpu.get_barrier_semaphore()
    for step in range(1, groups):
        pl.semaphore_signal(
            barrier, inc=1, device_id=(lax.rem(me + step, groups), my_mem), device_id_type=MESH
        )
    for step in range(1, members):
        pl.semaphore_signal(
            barrier, inc=1, device_id=(me, lax.rem(my_mem + step, members)), device_id_type=MESH
        )

    staged[...] = jnp.zeros_like(staged)

    def stage(first, last):
        for row in range(first, last):
            staged[pl.ds(row, stored, stride=SEND_ROWS), :] = bank[
                :, row * LANES : (row + 1) * LANES
            ]

    def part_for(group, part):
        picked = jnp.zeros((PART_ROWS, LANES), F32)
        for s in range(stored):
            first = s * SEND_ROWS + part * PART_ROWS
            rows = staged[first : first + PART_ROWS, :]
            picked = jnp.where(dest_ref[0, s] == group, rows, picked)
        return picked.astype(BF16)

    def fill(part):
        for step in range(1, groups):
            outbox[part, step] = part_for(lax.rem(me + step, groups), part)
        arrived[part, me] = part_for(me, part)

    def routed(part, step, source, group):
        return pltpu.make_async_remote_copy(
            src_ref=outbox.at[part, step],
            dst_ref=arrived.at[part, source],
            send_sem=out_send.at[part, step],
            recv_sem=out_recv.at[part, source],
            device_id=(group, my_mem),
            device_id_type=MESH,
        )

    sends = []

    def send(part):
        for step in range(1, groups):
            copy = routed(part, step, me, lax.rem(me + step, groups))
            copy.start()
            sends.append(copy)

    def place(part, slot):
        start = pl.multiple_of(slot * SLOT_ROWS + LEAD + part * PART_ROWS, 8)
        slots[pl.ds(start, PART_ROWS), :] = arrived[part, slot].astype(F32)

    def receive(part):
        place(part, me)
        for step in range(1, groups):
            source = lax.rem(me + groups - step, groups)
            routed(part, step, source, source).wait_recv()
            place(part, source)

    loads[0].wait()
    stage(0, PART_ROWS)
    fill(0)
    pl.semaphore_wait(barrier, groups - 1 + members - 1)
    send(0)
    stage(PART_ROWS, FLAT_ROWS)
    fill(1)
    send(1)
    for load in loads[1:]:
        load.start()

    slots[...] = jnp.zeros_like(slots)
    w0[w0_hbm.shape[0] :, :] = jnp.zeros((WINDOW - w0_hbm.shape[0], channels), BF16)
    halo = 2 * groups
    half = rows_all // 2
    for buffer in (ping, pong):
        buffer[0, half:, :] = jnp.zeros((halo, LANES), BF16)
        buffer[1, :halo, :] = jnp.zeros((halo, LANES), BF16)
    empty = jnp.zeros((SCALE - 1, LANES, LANES), BF16)
    branch[:, 3 * LANES :, :LANES] = empty
    branch[:, :LANES, LANES:] = empty
    back[...] = jnp.zeros_like(back)

    lane = lax.broadcasted_iota(jnp.int32, (groups, LANES), 1)

    def windows(block, _, phases=range(8)):
        first = block * 5
        held = {}

        def row_at(index):
            if index not in held:
                held[index] = slots[pl.ds(first + index, groups, stride=SLOT_ROWS), :]
            return held[index]

        pair = []
        for phase in phases:
            begin = phase * MELS + LEAD * LANES - 2 * MELS
            index, offset = begin // LANES, begin % LANES
            pieces = []
            for j in range(4):
                low = row_at(index + j)
                if offset:
                    high = row_at(index + j + 1) if j < 3 else None
                    low = pltpu.roll(low, LANES - offset, 1)
                    if high is not None:
                        high = pltpu.roll(high, LANES - offset, 1)
                        low = jnp.where(lane < LANES - offset, low, high)
                if j == 3:
                    low = jnp.where(lane < TAPS0 * MELS - 3 * LANES, low, 0.0)
                pieces.append(low)
            pair.append(jnp.concatenate(pieces, axis=1))
            if len(pair) == 2:
                side, place_in = phase // 2 % 2, phase // 4
                start = pl.multiple_of(side * half + (block * 2 + place_in) * halo, 16)
                cols[pl.ds(start, 2 * groups), :] = jnp.concatenate(pair, axis=0).astype(BF16)
                pair = []
        return 0


    chunks = [slice(c, c + CHUNK) for c in range(0, channels, CHUNK)]
    narrow = [slice(c, c + LANES) for c in range(0, channels, LANES)]
    half_tiles = tiles // 2
    part_tiles = half_tiles // 2

    def first_layers(step, _, part):
        side = step // part_tiles
        start = side * half_tiles + part * part_tiles + step % part_tiles
        rows_of_tile(side, start)
        return 0

    def rows_of_tile(side, tile):
        rows = pl.ds(pl.multiple_of(tile * TILE, 16), TILE)
        for chunk in chunks:
            out = jnp.maximum(dot(cols[rows, :], w0[:, chunk]), 0.0)
            front[rows, chunk] = out.astype(BF16)
        start = pl.multiple_of(tile % half_tiles * TILE + side * halo, 16)
        for chunk in chunks:
            expanded = jnp.maximum(dot(front[rows, :], expand[:, chunk]), 0.0).astype(BF16)
            work[rows, chunk] = expanded
            if chunk.start == 0:
                ping[side, pl.ds(start, TILE), :] = expanded[:, LANES : 2 * LANES]

    split = FRAMES // 16
    receive(0)
    lax.fori_loop(0, split, windows, 0)
    windows(split, 0, range(4))
    loads[1].wait()
    loads[2].wait()
    lax.fori_loop(0, half_tiles, functools.partial(first_layers, part=0), 0)
    receive(1)
    windows(split, 0, range(4, 8))
    lax.fori_loop(split + 1, FRAMES // 8, windows, 0)
    lax.fori_loop(0, half_tiles, functools.partial(first_layers, part=1), 0)

    loads[3].wait()
    loads[4].wait()
    buffers = (ping, pong)
    for i in range(1, SCALE):
        source, target = buffers[(i - 1) % 2], buffers[i % 2]

        def one_branch(tile, _, i=i, source=source, target=target):
            start = pl.multiple_of(tile * TILE, 16)
            near, far = pl.ds(start, TILE), pl.ds(start + halo, TILE)
            window = jnp.concatenate(
                [source[1, near, :], source[0, near, :], source[1, far, :], source[0, far, :]], axis=1
            )
            out = jnp.maximum(dot(window, branch[i - 1]), 0.0).astype(BF16)
            for side, spot in ((0, near), (1, far)):
                rows = pl.ds(start + side * half, TILE)
                mine = out[:, side * LANES : (side + 1) * LANES]
                work[rows, i * LANES : (i + 1) * LANES] = mine
                if i < SCALE - 1:
                    following = work[rows, (i + 1) * LANES : (i + 2) * LANES].astype(F32)
                    target[side, spot, :] = (following + mine.astype(F32)).astype(BF16)
            return 0

        lax.fori_loop(0, half_tiles, one_branch, 0, unroll=True)

    loads[5].wait()

    def by_frame(values):
        return values.reshape(values.shape[0] // groups, groups, values.shape[1])

    def merging(tile, total):
        rows = pl.ds(pl.multiple_of(tile * TILE, 16), TILE)
        sums = []
        for chunk in chunks:
            merged = jnp.maximum(dot(work[rows, :], merge[:, chunk]), 0.0)
            wide[rows, chunk] = merged
            sums.append(jnp.sum(by_frame(merged), axis=0))
        return total + jnp.concatenate(sums, axis=1)

    zeros = jnp.zeros((groups, channels), F32)
    total = lax.fori_loop(0, tiles, merging, zeros)

    loads[6].wait()
    loads[7].wait()
    hidden = jnp.maximum(dot_split(total / FRAMES, squeeze[...]), 0.0)
    excited = 1.0 / (1.0 + jnp.exp(-dot_split(hidden, excite[...])))

    loads[8].wait()
    pivot = front[0 : 2 * groups, :].astype(F32)[:groups] + wide[0:groups, :] * excited

    def trunk_out(tile, carry):
        first, second = carry
        rows = pl.ds(pl.multiple_of(tile * TILE, 16), TILE)
        sums, squares = [], []
        for chunk in narrow:
            out = by_frame(wide[rows, chunk]) * excited[:, chunk]
            out = by_frame(front[rows, chunk].astype(F32)) + out
            work[rows, chunk] = out.reshape(TILE, LANES).astype(BF16)
            moved = out - pivot[:, chunk]
            sums.append(jnp.sum(moved, axis=0))
            squares.append(jnp.sum(moved * moved, axis=0))
        attn[rows, :] = dot(work[rows, :], attend[0:channels, :])
        return first + jnp.concatenate(sums, axis=1), second + jnp.concatenate(squares, axis=1)

    first, second = lax.fori_loop(0, tiles, trunk_out, (zeros, zeros))
    shift = first / FRAMES
    center = pivot + shift
    spread = jnp.sqrt(jnp.maximum(second / FRAMES - shift * shift, 0.0) + EPS_STAT)
    context = dot_split(center, attend[channels : 2 * channels, :]) + dot_split(
        spread, attend[2 * channels :, :]
    )

    loads[9].wait()

    inverse = 1.0 / spread

    def energies(tile, carry):
        rows = pl.ds(pl.multiple_of(tile * TILE, 16), TILE)
        attended = jnp.tanh(by_frame(attn[rows, :]) + context).reshape(TILE, -1).astype(BF16)
        parts = ([], [], [])
        for chunk in chunks:
            weights = by_frame(jnp.exp(dot(attended, score[:, chunk])))
            value = by_frame(work[rows, chunk].astype(F32))
            value = (value - center[:, chunk]) * inverse[:, chunk]
            parts[0].append(jnp.sum(weights, axis=0))
            weights = weights * value
            parts[1].append(jnp.sum(weights, axis=0))
            parts[2].append(jnp.sum(weights * value, axis=0))
        return tuple(c + jnp.concatenate(p, axis=1) for c, p in zip(carry, parts))

    norm, weighted, squared = lax.fori_loop(0, tiles, energies, (zeros, zeros, zeros))
    weighted = weighted / norm
    squared = jnp.maximum(squared / norm - weighted * weighted, 0.0)
    mean = center + spread * weighted
    deviation = jnp.sqrt(spread * spread * squared + EPS_STAT)

    loads[10].wait()
    loads[11].wait()
    pooled = jnp.concatenate([mean, deviation], axis=1).astype(BF16)
    embedding = lax.dot_general(
        pooled, embed[...], (((1,), (1,)), ((), ())), preferred_element_type=F32
    )
    scores = dot(embedding.astype(BF16), lang[...])
    width = embedding.shape[1]
    langs = scores.shape[1]
    back[:, 0, :] = embedding[:, :LANES]
    back[:, 1, : width - LANES] = embedding[:, LANES:]
    back[:, 2, :langs] = scores

    for step in range(1, groups):
        group = lax.rem(me + step, groups)
        copy = pltpu.make_async_remote_copy(
            src_ref=back.at[group],
            dst_ref=home.at[me],
            send_sem=back_send.at[step],
            recv_sem=back_recv.at[me],
            device_id=(group, my_mem),
            device_id_type=MESH,
        )
        copy.start()
        sends.append(copy)
    home[me] = back[me]
    for step in range(1, groups):
        source = lax.rem(me + groups - step, groups)
        pltpu.make_async_remote_copy(
            src_ref=back.at[source],
            dst_ref=home.at[source],
            send_sem=back_send.at[step],
            recv_sem=back_recv.at[source],
            device_id=(source, my_mem),
            device_id_type=MESH,
        ).wait_recv()
    for s in range(stored):
        picked = home[0]
        for group in range(1, groups):
            picked = jnp.where(dest_ref[0, s] == group, home[group], picked)
        own[s] = picked

    left, right = own[:, 0, :], own[:, 1, :]
    result_ref[:, :LANES] = own[:, 2, :]
    squares = jnp.sum(left * left + right * right, axis=1, keepdims=True)
    factor = lax.rsqrt(squares / width + EPS_NORM)
    mine = jnp.concatenate([left * factor, right * factor], axis=1).astype(BF16)
    normed[...] = mine.astype(F32)
    for step in range(1, members):
        member = lax.rem(my_mem + step, members)
        copy = pltpu.make_async_remote_copy(
            src_ref=normed,
            dst_ref=gathered.at[my_mem],
            send_sem=mem_send.at[step],
            recv_sem=mem_recv.at[my_mem],
            device_id=(me, member),
            device_id_type=MESH,
        )
        copy.start()
        sends.append(copy)
    gathered[my_mem] = normed[...]
    for step in range(1, members):
        source = lax.rem(my_mem + members - step, members)
        pltpu.make_async_remote_copy(
            src_ref=normed,
            dst_ref=gathered.at[source],
            send_sem=mem_send.at[step],
            recv_sem=mem_recv.at[source],
            device_id=(me, source),
            device_id_type=MESH,
        ).wait_recv()
    every = gathered[...].reshape(members * stored, 2 * LANES).astype(BF16)
    inner = lax.dot_general(mine, every, (((1,), (1,)), ((), ())), preferred_element_type=F32)
    result_ref[:, LANES : LANES + members * stored] = inner / width
    for copy in sends:
        copy.wait_send()


def split_result(result_ref, logits_ref, sim_ref):
    logits_ref[0] = result_ref[:, : logits_ref.shape[2]]
    sim_ref[0] = result_ref[:, LANES : LANES + sim_ref.shape[2]]


def shards(
    filterbank,
    destination,
    initial_conv_weight,
    expand_weight,
    branch_weight,
    merge_weight,
    squeeze_weight,
    excite_weight,
    attend_weight,
    score_weight,
    embed_weight,
    language_weight,
):
    groups = lax.axis_size("grp")
    members = lax.axis_size("mem")
    stored = filterbank.shape[2]
    rows = FRAMES * groups
    channels = expand_weight.shape[0]
    langs = language_weight.shape[2]
    operands = (
        filterbank.reshape(stored, FRAMES * MELS),
        destination,
        initial_conv_weight,
        expand_weight,
        branch_weight,
        merge_weight,
        squeeze_weight,
        excite_weight,
        attend_weight[0],
        score_weight[0],
        embed_weight[0].T,
        language_weight[0],
    )
    copied = [pltpu.VMEM(a.shape, a.dtype) for a in operands]
    del copied[1]
    copied[1] = pltpu.VMEM((WINDOW, channels), BF16)
    copied[3] = pltpu.VMEM((SCALE - 1, 4 * LANES, 2 * LANES), BF16)
    anywhere = pl.BlockSpec(memory_space=pl.ANY)
    in_specs = [anywhere] * len(operands)
    in_specs[1] = pl.BlockSpec(memory_space=pltpu.SMEM)
    dma = pltpu.SemaphoreType.DMA
    result = pl.pallas_call(
        functools.partial(kernel, groups, members),
        out_shape=jax.ShapeDtypeStruct((stored, 2 * LANES), F32),
        in_specs=in_specs,
        out_specs=pl.BlockSpec(memory_space=pltpu.VMEM),
        scratch_shapes=copied
        + [
            pltpu.VMEM((stored * SEND_ROWS, LANES), F32),
            pltpu.VMEM((2, groups, PART_ROWS, LANES), BF16),
            pltpu.VMEM((2, groups, PART_ROWS, LANES), BF16),
            pltpu.VMEM((groups * SLOT_ROWS, LANES), F32),
            pltpu.VMEM((rows, WINDOW), BF16),
            pltpu.VMEM((rows, channels), BF16),
            pltpu.VMEM((rows, channels), BF16),
            pltpu.VMEM((rows, channels), F32),
            pltpu.VMEM((2, rows // 2 + 2 * groups, LANES), BF16),
            pltpu.VMEM((2, rows // 2 + 2 * groups, LANES), BF16),
            pltpu.VMEM((rows, LANES), F32),
            pltpu.VMEM((groups, 8, LANES), F32),
            pltpu.VMEM((groups, 8, LANES), F32),
            pltpu.VMEM((stored, 8, LANES), F32),
            pltpu.VMEM((stored, 2 * LANES), F32),
            pltpu.VMEM((members, stored, 2 * LANES), F32),
            dma((len(copied) + 1,)),
            dma((2, groups)),
            dma((2, groups)),
            dma((groups,)),
            dma((groups,)),
            dma((members,)),
            dma((members,)),
        ],
        compiler_params=pltpu.CompilerParams(
            collective_id=0, has_side_effects=True, vmem_limit_bytes=60 * 1024 * 1024
        ),
        cost_estimate=pl.CostEstimate(
            flops=rows * 12_000_000, bytes_accessed=10_000_000, transcendentals=rows * 1200
        ),
    )(*operands)
    return pl.pallas_call(
        split_result,
        out_shape=(
            jax.ShapeDtypeStruct((1, stored, langs), F32),
            jax.ShapeDtypeStruct((1, stored, members * stored), F32),
        ),
    )(result)


def solution(mesh):
    return jax.shard_map(
        shards,
        mesh=mesh,
        in_specs=(
            P("grp", "mem", None, None),
            P("grp", "mem"),
            P(),
            P(),
            P(),
            P(),
            P(),
            P(),
            P("grp", None, None),
            P("grp", None, None),
            P("grp", None, None),
            P("grp", None, None),
        ),
        out_specs=(P("grp", "mem", None), P("grp", "mem", None)),
        check_vma=False,
    )
```

```python
import functools

import jax
import jax.numpy as jnp
from jax import lax
from jax.experimental import pallas as pl
from jax.experimental.pallas import tpu as pltpu
from jax.sharding import PartitionSpec as P

MELS = 80
SCALE = 8
FRAMES = 200
LANES = 128
FLAT_ROWS = 125
PART_ROWS = 64
SEND_ROWS = 128
LEAD = 8
SLOT_ROWS = LEAD + SEND_ROWS
TAPS0 = 5
WINDOW = 512
TILE = 400
CHUNK = 256
EPS_STAT = 1e-05
EPS_NORM = 1e-06

MESH = pl.DeviceIdType.MESH
F32 = jnp.float32
BF16 = jnp.bfloat16


def dot(a, b):
    return jnp.dot(a, b, preferred_element_type=F32)


def dot_split(values, weight):
    rows = values.shape[0]
    high = values.astype(BF16).astype(F32)
    both = jnp.concatenate([high, values - high], axis=0).astype(BF16)
    product = dot(both, weight)
    return product[:rows] + product[rows:]


def kernel(
    groups,
    members,
    bank_hbm,
    dest_ref,
    w0_hbm,
    expand_hbm,
    branch_hbm,
    merge_hbm,
    squeeze_hbm,
    excite_hbm,
    attend_hbm,
    score_hbm,
    embed_hbm,
    lang_hbm,
    result_ref,
    bank,
    w0,
    expand,
    branch,
    merge,
    squeeze,
    excite,
    attend,
    score,
    embed,
    lang,
    staged,
    outbox,
    arrived,
    slots,
    cols,
    front,
    work,
    wide,
    ping,
    pong,
    attn,
    back,
    home,
    own,
    normed,
    gathered,
    load_sem,
    out_send,
    out_recv,
    back_send,
    back_recv,
    mem_send,
    mem_recv,
):
    stored = bank.shape[0]
    rows_all = FRAMES * groups
    tiles = rows_all // TILE
    channels = front.shape[1]
    me = lax.axis_index("grp")
    my_mem = lax.axis_index("mem")

    pairs = [
        (bank_hbm, bank),
        (w0_hbm, w0.at[pl.ds(0, w0_hbm.shape[0])]),
        (expand_hbm, expand),
        (branch_hbm, branch.at[:, pl.ds(0, 3 * LANES), pl.ds(0, LANES)]),
        (branch_hbm, branch.at[:, pl.ds(LANES, 3 * LANES), pl.ds(LANES, LANES)]),
        (merge_hbm, merge),
        (squeeze_hbm, squeeze),
        (excite_hbm, excite),
        (attend_hbm, attend),
        (score_hbm, score),
        (embed_hbm, embed),
        (lang_hbm, lang),
    ]
    loads = [
        pltpu.make_async_copy(source, target, load_sem.at[i])
        for i, (source, target) in enumerate(pairs)
    ]
    loads[0].start()

    barrier = pltpu.get_barrier_semaphore()
    for step in range(1, groups):
        pl.semaphore_signal(
            barrier, inc=1, device_id=(lax.rem(me + step, groups), my_mem), device_id_type=MESH
        )
    for step in range(1, members):
        pl.semaphore_signal(
            barrier, inc=1, device_id=(me, lax.rem(my_mem + step, members)), device_id_type=MESH
        )

    staged[...] = jnp.zeros_like(staged)

    def stage(first, last):
        for row in range(first, last):
            staged[pl.ds(row, stored, stride=SEND_ROWS), :] = bank[
                :, row * LANES : (row + 1) * LANES
            ]

    def part_for(group, part):
        picked = jnp.zeros((PART_ROWS, LANES), F32)
        for s in range(stored):
            first = s * SEND_ROWS + part * PART_ROWS
            rows = staged[first : first + PART_ROWS, :]
            picked = jnp.where(dest_ref[0, s] == group, rows, picked)
        return picked.astype(BF16)

    def fill(part):
        for step in range(1, groups):
            outbox[part, step] = part_for(lax.rem(me + step, groups), part)
        arrived[part, me] = part_for(me, part)

    def routed(part, step, source, group):
        return pltpu.make_async_remote_copy(
            src_ref=outbox.at[part, step],
            dst_ref=arrived.at[part, source],
            send_sem=out_send.at[part, step],
            recv_sem=out_recv.at[part, source],
            device_id=(group, my_mem),
            device_id_type=MESH,
        )

    sends = []

    def send(part):
        for step in range(1, groups):
            copy = routed(part, step, me, lax.rem(me + step, groups))
            copy.start()
            sends.append(copy)

    def place(part, slot):
        start = pl.multiple_of(slot * SLOT_ROWS + LEAD + part * PART_ROWS, 8)
        slots[pl.ds(start, PART_ROWS), :] = arrived[part, slot].astype(F32)

    def receive(part):
        place(part, me)
        for step in range(1, groups):
            source = lax.rem(me + groups - step, groups)
            routed(part, step, source, source).wait_recv()
            place(part, source)

    loads[0].wait()
    stage(0, PART_ROWS)
    fill(0)
    pl.semaphore_wait(barrier, groups - 1 + members - 1)
    send(0)
    stage(PART_ROWS, FLAT_ROWS)
    fill(1)
    send(1)
    for load in loads[1:]:
        load.start()

    slots[...] = jnp.zeros_like(slots)
    w0[w0_hbm.shape[0] :, :] = jnp.zeros((WINDOW - w0_hbm.shape[0], channels), BF16)
    halo = 2 * groups
    half = rows_all // 2
    for buffer in (ping, pong):
        buffer[0, half:, :] = jnp.zeros((halo, LANES), BF16)
        buffer[1, :halo, :] = jnp.zeros((halo, LANES), BF16)
    empty = jnp.zeros((SCALE - 1, LANES, LANES), BF16)
    branch[:, 3 * LANES :, :LANES] = empty
    branch[:, :LANES, LANES:] = empty
    back[...] = jnp.zeros_like(back)

    lane = lax.broadcasted_iota(jnp.int32, (groups, LANES), 1)

    def windows(block, _, phases=range(8)):
        first = block * 5
        held = {}

        def row_at(index):
            if index not in held:
                held[index] = slots[pl.ds(first + index, groups, stride=SLOT_ROWS), :]
            return held[index]

        pair = []
        for phase in phases:
            begin = phase * MELS + LEAD * LANES - 2 * MELS
            index, offset = begin // LANES, begin % LANES
            pieces = []
            for j in range(4):
                low = row_at(index + j)
                if offset:
                    high = row_at(index + j + 1) if j < 3 else None
                    low = pltpu.roll(low, LANES - offset, 1)
                    if high is not None:
                        high = pltpu.roll(high, LANES - offset, 1)
                        low = jnp.where(lane < LANES - offset, low, high)
                if j == 3:
                    low = jnp.where(lane < TAPS0 * MELS - 3 * LANES, low, 0.0)
                pieces.append(low)
            pair.append(jnp.concatenate(pieces, axis=1))
            if len(pair) == 2:
                side, place_in = phase // 2 % 2, phase // 4
                start = pl.multiple_of(side * half + (block * 2 + place_in) * halo, 16)
                cols[pl.ds(start, 2 * groups), :] = jnp.concatenate(pair, axis=0).astype(BF16)
                pair = []
        return 0


    chunks = [slice(c, c + CHUNK) for c in range(0, channels, CHUNK)]
    narrow = [slice(c, c + LANES) for c in range(0, channels, LANES)]
    half_tiles = tiles // 2
    part_tiles = half_tiles // 2

    def first_layers(step, _, part):
        side = step // part_tiles
        start = side * half_tiles + part * part_tiles + step % part_tiles
        rows_of_tile(side, start)
        return 0

    def rows_of_tile(side, tile):
        rows = pl.ds(pl.multiple_of(tile * TILE, 16), TILE)
        out = jnp.maximum(dot(cols[rows, :], w0[...]), 0.0).astype(BF16)
        front[rows, :] = out
        start = pl.multiple_of(tile % half_tiles * TILE + side * halo, 16)
        expanded = jnp.maximum(dot(out, expand[...]), 0.0).astype(BF16)
        work[rows, :] = expanded
        ping[side, pl.ds(start, TILE), :] = expanded[:, LANES : 2 * LANES]

    split = FRAMES // 16
    receive(0)
    lax.fori_loop(0, split, windows, 0)
    windows(split, 0, range(4))
    loads[1].wait()
    loads[2].wait()
    lax.fori_loop(0, half_tiles, functools.partial(first_layers, part=0), 0)
    receive(1)
    windows(split, 0, range(4, 8))
    lax.fori_loop(split + 1, FRAMES // 8, windows, 0)
    lax.fori_loop(0, half_tiles, functools.partial(first_layers, part=1), 0)

    loads[3].wait()
    loads[4].wait()
    buffers = (ping, pong)
    for i in range(1, SCALE):
        source, target = buffers[(i - 1) % 2], buffers[i % 2]

        def one_branch(tile, _, i=i, source=source, target=target):
            start = pl.multiple_of(tile * TILE, 16)
            near, far = pl.ds(start, TILE), pl.ds(start + halo, TILE)
            window = jnp.concatenate(
                [source[1, near, :], source[0, near, :], source[1, far, :], source[0, far, :]], axis=1
            )
            out = jnp.maximum(dot(window, branch[i - 1]), 0.0).astype(BF16)
            for side, spot in ((0, near), (1, far)):
                rows = pl.ds(start + side * half, TILE)
                mine = out[:, side * LANES : (side + 1) * LANES]
                work[rows, i * LANES : (i + 1) * LANES] = mine
                if i < SCALE - 1:
                    following = work[rows, (i + 1) * LANES : (i + 2) * LANES].astype(F32)
                    target[side, spot, :] = (following + mine.astype(F32)).astype(BF16)
            return 0

        lax.fori_loop(0, half_tiles, one_branch, 0, unroll=True)

    loads[5].wait()

    def by_frame(values):
        return values.reshape(values.shape[0] // groups, groups, values.shape[1])

    def merging(tile, total):
        rows = pl.ds(pl.multiple_of(tile * TILE, 16), TILE)
        merged = jnp.maximum(dot(work[rows, :], merge[...]), 0.0)
        wide[rows, :] = merged
        return total + jnp.sum(by_frame(merged), axis=0)

    zeros = jnp.zeros((groups, channels), F32)
    total = lax.fori_loop(0, tiles, merging, zeros)

    loads[6].wait()
    loads[7].wait()
    hidden = jnp.maximum(dot_split(total / FRAMES, squeeze[...]), 0.0)
    excited = 1.0 / (1.0 + jnp.exp(-dot_split(hidden, excite[...])))

    loads[8].wait()
    pivot = front[0 : 2 * groups, :].astype(F32)[:groups] + wide[0:groups, :] * excited

    def trunk_out(tile, carry):
        first, second = carry
        rows = pl.ds(pl.multiple_of(tile * TILE, 16), TILE)
        sums, squares = [], []
        for chunk in narrow:
            out = by_frame(wide[rows, chunk]) * excited[:, chunk]
            out = by_frame(front[rows, chunk].astype(F32)) + out
            work[rows, chunk] = out.reshape(TILE, LANES).astype(BF16)
            moved = out - pivot[:, chunk]
            sums.append(jnp.sum(moved, axis=0))
            squares.append(jnp.sum(moved * moved, axis=0))
        attn[rows, :] = dot(work[rows, :], attend[0:channels, :])
        return first + jnp.concatenate(sums, axis=1), second + jnp.concatenate(squares, axis=1)

    first, second = lax.fori_loop(0, tiles, trunk_out, (zeros, zeros))
    shift = first / FRAMES
    center = pivot + shift
    spread = jnp.sqrt(jnp.maximum(second / FRAMES - shift * shift, 0.0) + EPS_STAT)
    context = dot_split(center, attend[channels : 2 * channels, :]) + dot_split(
        spread, attend[2 * channels :, :]
    )

    loads[9].wait()

    inverse = 1.0 / spread

    def energies(tile, carry):
        rows = pl.ds(pl.multiple_of(tile * TILE, 16), TILE)
        attended = jnp.tanh(by_frame(attn[rows, :]) + context).reshape(TILE, -1).astype(BF16)
        parts = ([], [], [])
        for chunk in chunks:
            weights = by_frame(jnp.exp(dot(attended, score[:, chunk])))
            value = by_frame(work[rows, chunk].astype(F32))
            value = (value - center[:, chunk]) * inverse[:, chunk]
            parts[0].append(jnp.sum(weights, axis=0))
            weights = weights * value
            parts[1].append(jnp.sum(weights, axis=0))
            parts[2].append(jnp.sum(weights * value, axis=0))
        return tuple(c + jnp.concatenate(p, axis=1) for c, p in zip(carry, parts))

    norm, weighted, squared = lax.fori_loop(0, tiles, energies, (zeros, zeros, zeros))
    weighted = weighted / norm
    squared = jnp.maximum(squared / norm - weighted * weighted, 0.0)
    mean = center + spread * weighted
    deviation = jnp.sqrt(spread * spread * squared + EPS_STAT)

    loads[10].wait()
    loads[11].wait()
    pooled = jnp.concatenate([mean, deviation], axis=1).astype(BF16)
    embedding = lax.dot_general(
        pooled, embed[...], (((1,), (1,)), ((), ())), preferred_element_type=F32
    )
    scores = dot(embedding.astype(BF16), lang[...])
    width = embedding.shape[1]
    langs = scores.shape[1]
    back[:, 0, :] = embedding[:, :LANES]
    back[:, 1, : width - LANES] = embedding[:, LANES:]
    back[:, 2, :langs] = scores

    for step in range(1, groups):
        group = lax.rem(me + step, groups)
        copy = pltpu.make_async_remote_copy(
            src_ref=back.at[group],
            dst_ref=home.at[me],
            send_sem=back_send.at[step],
            recv_sem=back_recv.at[me],
            device_id=(group, my_mem),
            device_id_type=MESH,
        )
        copy.start()
        sends.append(copy)
    home[me] = back[me]
    for step in range(1, groups):
        source = lax.rem(me + groups - step, groups)
        pltpu.make_async_remote_copy(
            src_ref=back.at[source],
            dst_ref=home.at[source],
            send_sem=back_send.at[step],
            recv_sem=back_recv.at[source],
            device_id=(source, my_mem),
            device_id_type=MESH,
        ).wait_recv()
    for s in range(stored):
        picked = home[0]
        for group in range(1, groups):
            picked = jnp.where(dest_ref[0, s] == group, home[group], picked)
        own[s] = picked

    left, right = own[:, 0, :], own[:, 1, :]
    result_ref[:, :LANES] = own[:, 2, :]
    squares = jnp.sum(left * left + right * right, axis=1, keepdims=True)
    factor = lax.rsqrt(squares / width + EPS_NORM)
    mine = jnp.concatenate([left * factor, right * factor], axis=1).astype(BF16)
    normed[...] = mine.astype(F32)
    for step in range(1, members):
        member = lax.rem(my_mem + step, members)
        copy = pltpu.make_async_remote_copy(
            src_ref=normed,
            dst_ref=gathered.at[my_mem],
            send_sem=mem_send.at[step],
            recv_sem=mem_recv.at[my_mem],
            device_id=(me, member),
            device_id_type=MESH,
        )
        copy.start()
        sends.append(copy)
    gathered[my_mem] = normed[...]
    for step in range(1, members):
        source = lax.rem(my_mem + members - step, members)
        pltpu.make_async_remote_copy(
            src_ref=normed,
            dst_ref=gathered.at[source],
            send_sem=mem_send.at[step],
            recv_sem=mem_recv.at[source],
            device_id=(me, source),
            device_id_type=MESH,
        ).wait_recv()
    every = gathered[...].reshape(members * stored, 2 * LANES).astype(BF16)
    inner = lax.dot_general(mine, every, (((1,), (1,)), ((), ())), preferred_element_type=F32)
    result_ref[:, LANES : LANES + members * stored] = inner / width
    for copy in sends:
        copy.wait_send()


def split_result(result_ref, logits_ref, sim_ref):
    logits_ref[0] = result_ref[:, : logits_ref.shape[2]]
    sim_ref[0] = result_ref[:, LANES : LANES + sim_ref.shape[2]]


def shards(
    filterbank,
    destination,
    initial_conv_weight,
    expand_weight,
    branch_weight,
    merge_weight,
    squeeze_weight,
    excite_weight,
    attend_weight,
    score_weight,
    embed_weight,
    language_weight,
):
    groups = lax.axis_size("grp")
    members = lax.axis_size("mem")
    stored = filterbank.shape[2]
    rows = FRAMES * groups
    channels = expand_weight.shape[0]
    langs = language_weight.shape[2]
    operands = (
        filterbank.reshape(stored, FRAMES * MELS),
        destination,
        initial_conv_weight,
        expand_weight,
        branch_weight,
        merge_weight,
        squeeze_weight,
        excite_weight,
        attend_weight[0],
        score_weight[0],
        embed_weight[0].T,
        language_weight[0],
    )
    copied = [pltpu.VMEM(a.shape, a.dtype) for a in operands]
    del copied[1]
    copied[1] = pltpu.VMEM((WINDOW, channels), BF16)
    copied[3] = pltpu.VMEM((SCALE - 1, 4 * LANES, 2 * LANES), BF16)
    anywhere = pl.BlockSpec(memory_space=pl.ANY)
    in_specs = [anywhere] * len(operands)
    in_specs[1] = pl.BlockSpec(memory_space=pltpu.SMEM)
    dma = pltpu.SemaphoreType.DMA
    result = pl.pallas_call(
        functools.partial(kernel, groups, members),
        out_shape=jax.ShapeDtypeStruct((stored, 2 * LANES), F32),
        in_specs=in_specs,
        out_specs=pl.BlockSpec(memory_space=pltpu.VMEM),
        scratch_shapes=copied
        + [
            pltpu.VMEM((stored * SEND_ROWS, LANES), F32),
            pltpu.VMEM((2, groups, PART_ROWS, LANES), BF16),
            pltpu.VMEM((2, groups, PART_ROWS, LANES), BF16),
            pltpu.VMEM((groups * SLOT_ROWS, LANES), F32),
            pltpu.VMEM((rows, WINDOW), BF16),
            pltpu.VMEM((rows, channels), BF16),
            pltpu.VMEM((rows, channels), BF16),
            pltpu.VMEM((rows, channels), F32),
            pltpu.VMEM((2, rows // 2 + 2 * groups, LANES), BF16),
            pltpu.VMEM((2, rows // 2 + 2 * groups, LANES), BF16),
            pltpu.VMEM((rows, LANES), F32),
            pltpu.VMEM((groups, 8, LANES), F32),
            pltpu.VMEM((groups, 8, LANES), F32),
            pltpu.VMEM((stored, 8, LANES), F32),
            pltpu.VMEM((stored, 2 * LANES), F32),
            pltpu.VMEM((members, stored, 2 * LANES), F32),
            dma((len(copied) + 1,)),
            dma((2, groups)),
            dma((2, groups)),
            dma((groups,)),
            dma((groups,)),
            dma((members,)),
            dma((members,)),
        ],
        compiler_params=pltpu.CompilerParams(
            collective_id=0, has_side_effects=True, vmem_limit_bytes=60 * 1024 * 1024
        ),
        cost_estimate=pl.CostEstimate(
            flops=rows * 12_000_000, bytes_accessed=10_000_000, transcendentals=rows * 1200
        ),
    )(*operands)
    return pl.pallas_call(
        split_result,
        out_shape=(
            jax.ShapeDtypeStruct((1, stored, langs), F32),
            jax.ShapeDtypeStruct((1, stored, members * stored), F32),
        ),
    )(result)


def solution(mesh):
    return jax.shard_map(
        shards,
        mesh=mesh,
        in_specs=(
            P("grp", "mem", None, None),
            P("grp", "mem"),
            P(),
            P(),
            P(),
            P(),
            P(),
            P(),
            P("grp", None, None),
            P("grp", None, None),
            P("grp", None, None),
            P("grp", None, None),
        ),
        out_specs=(P("grp", "mem", None), P("grp", "mem", None)),
        check_vma=False,
    )
```
